128 devices in a mesh: tm: 32 (over z, x_hi, y), space: 4 (over x_lo, core).
Axes of the slice: x: 4 (x_hi: 2, x_lo: 2; x = x_hi * 2 + x_lo), y: 4, z: 4, core: 2. Of those that a mesh axis runs over, the one named last changes fastest.
Arguments:
- video_in: bfloat16 [32, 256, 64, 128], P('tm', 'space'), may hold values from -6 to 6
- cotangent: bfloat16 [32, 256, 64, 128], P('tm', 'space'), may hold values from -6 to 6
- kernel_a: bfloat16 [3, 3, 3, 64, 64], replicated, may hold values from -0.15625 to 0.15625
- kernel_b: bfloat16 [3, 3, 3, 64, 64], replicated, may hold values from -0.15625 to 0.15625
- plane_kernel: bfloat16 [3, 3, 64, 64], replicated, may hold values from -0.25 to 0.25
- plane_head: bfloat16 [64], replicated, may hold values from -0.75 to 0.75
- time_kernel: bfloat16 [3, 64, 64], replicated, may hold values from -0.4375 to 0.4375
- time_mixer: bfloat16 [64, 64], replicated, may hold values from -12 to 12
- time_head: bfloat16 [64], replicated, may hold values from -0.75 to 0.75
- listed: int32 [8], replicated, may hold values from 0 to 31, as said below
Outputs:
- video: bfloat16 [32, 256, 64, 128], P('tm', 'space')
- input_grad: bfloat16 [32, 256, 64, 128], P('tm', 'space')
- plane_scores: float32 [32, 4, 16, 128], P('tm', 'space')
- time_scores: float32 [4, 32, 64], P('space', 'tm')
The draws below stay inside these ranges and needn't reach their ends.
Inputs may be any that keep to these rules, and one draw needn't show every extreme that they name: `listed`: 8 distinct frame indices; the first is always frame 32 // 2, and frames 0 and 31 are always among the others, which stand in random order.
All inputs are finite; a program needn't handle non-finite values.
Results may differ from the reference program's by a relative error of at most 0.0053.
Values may be sent and summed in bfloat16 or wider, within the bound.
No kernel may reach another device: no remote copies, remote signals or barrier semaphores. Data moves between devices by JAX's collectives and lax.ppermute only.
A program may use at most 128 MiB of HBM per device.

```python
import jax
import jax.numpy as jnp
from jax import lax

C = 64
RD = 64
W = 128
LISTED = 8
NT = 32
H = 256
HPT = 32
WP = 64
N_TM = 32
N_SPACE = 4


def draw_listed(key, part):
    half_frame = NT // 2
    drawn = 1 + jax.random.permutation(jax.random.fold_in(key, 11), NT - 3)[:LISTED - 3]
    drawn = drawn.astype(jnp.int32)
    middle = jnp.where(drawn >= half_frame, drawn + 1, drawn)
    others = jnp.concatenate([jnp.array([0, NT - 1], jnp.int32), middle])
    shuffle = jax.random.permutation(jax.random.fold_in(key, 12), LISTED - 1)
    return jnp.concatenate([jnp.array([half_frame], jnp.int32), others[shuffle]])


def block_scale(own_key, shape, shards, low, top_value):
    factor_of, own = 1.0, jax.random.fold_in(own_key, 6)
    for position, parts in shards:
        steps = jnp.exp(jax.random.uniform(jax.random.fold_in(own, position), (parts,), jnp.float32, low / len(shards), top_value / len(shards)))
        factor_of = factor_of * jnp.repeat(steps, shape[position] // parts).reshape([-1 if axis == position else 1 for axis in range(len(shape))])
    return factor_of


def gaussian(stream_key, shape, spread, most, cuts=(), dtype=jnp.bfloat16):
    values = spread * jax.random.normal(stream_key, shape, jnp.float32)
    if cuts:
        values = values * block_scale(stream_key, shape, cuts, -0.22, 0.18)
    return jnp.clip(values, -most, most).astype(dtype)


def setup_inputs(seed: int = 0) -> dict:
    key_list = jax.random.split(jax.random.key(seed), 11)
    video_in = gaussian(key_list[0], (NT, H, C, W), 1.0, 6.0, ((0, 32), (1, 4)))
    cotangent = gaussian(key_list[1], (NT, H, C, W), 1.0, 6.0, ((0, 32), (1, 4)))
    kernel_a = gaussian(key_list[2], (3, 3, 3, C, C), (27 * C) ** -0.5, 0.15625)
    kernel_b = gaussian(key_list[3], (3, 3, 3, C, C), (27 * C) ** -0.5, 0.15625)
    plane_kernel = gaussian(key_list[4], (3, 3, C, C), (9 * C) ** -0.5, 0.25)
    plane_head = gaussian(key_list[5], (C,), C ** -0.5, 0.75)
    time_kernel = gaussian(key_list[6], (3, C, C), (3 * C) ** -0.5, 0.4375)
    time_mixer = gaussian(key_list[7], (C, C), (C ** -0.5 * 16), 12.0)
    time_head = gaussian(key_list[8], (C,), C ** -0.5, 0.75)
    listed = draw_listed(jax.random.fold_in(key_list[10], 71), 0)
    return {"video_in": video_in, "cotangent": cotangent, "kernel_a": kernel_a, "kernel_b": kernel_b, "plane_kernel": plane_kernel, "plane_head": plane_head, "time_kernel": time_kernel, "time_mixer": time_mixer, "time_head": time_head, "listed": listed}


def cube_conv(volume, kernel):
    padded = jnp.pad(volume.astype(jnp.float32), ((1, 1), (1, 1), (0, 0), (0, 0)))
    return lax.conv_general_dilated(padded[None], kernel.astype(jnp.float32), (1, 1, 1), [(0, 0), (0, 0), (1, 1)], dimension_numbers=("NDHCW", "DHWIO", "NDHCW"), precision=lax.Precision.HIGHEST)[0]


def flipped(kernel):
    return jnp.swapaxes(kernel[::-1, ::-1, ::-1], 3, 4)


def silu_slope(values):
    logistic = jax.nn.sigmoid(values)
    return logistic * (1.0 + values * (1.0 - logistic))


def plane_map(frames, kernel, head):
    padded = jnp.pad(frames.astype(jnp.float32), ((0, 0), (1, 1), (0, 0), (0, 0)))
    conv_out = lax.conv_general_dilated(padded, kernel.astype(jnp.float32), (1, 1), [(0, 0), (1, 1)], dimension_numbers=("NHCW", "HWIO", "NHCW"), precision=lax.Precision.HIGHEST)
    return jnp.einsum("nhow,o->nhw", jax.nn.silu(conv_out), head.astype(jnp.float32), precision=lax.Precision.HIGHEST)


def pool_pairs(volume):
    shaped = volume.astype(jnp.float32).reshape(volume.shape[0], volume.shape[1] // 2, 2, volume.shape[2], volume.shape[3] // 2, 2)
    return jnp.mean(shaped, axis=(2, 5)).astype(jnp.bfloat16)


def time_conv(rimmed, kernel):
    length = rimmed.shape[0] - 2
    total = jnp.zeros((length, rimmed.shape[1], kernel.shape[2], rimmed.shape[3]), jnp.float32)
    for offset in range(3):
        total = total + jnp.einsum("thcw,co->thow", rimmed[offset:offset + length].astype(jnp.float32), kernel[offset].astype(jnp.float32), precision=lax.Precision.HIGHEST)
    return total


def time_head_map(time_mean, mixer, head):
    mixed_units = jnp.einsum("hcw,co->how", time_mean, mixer.astype(jnp.float32), precision=lax.Precision.HIGHEST)
    return jnp.einsum("how,o->hw", jax.nn.silu(mixed_units), head.astype(jnp.float32), precision=lax.Precision.HIGHEST)


def reference(video_in, cotangent, kernel_a, kernel_b, plane_kernel, plane_head, time_kernel, time_mixer, time_head, listed):
    float_in = video_in.astype(jnp.float32)
    hidden_in = jax.nn.silu(float_in).astype(jnp.bfloat16)
    pre_act = cube_conv(hidden_in, kernel_a)
    inner_act = jax.nn.silu(pre_act).astype(jnp.bfloat16)
    generated = (float_in + cube_conv(inner_act, kernel_b)).astype(jnp.bfloat16)
    grad_pre = (cube_conv(cotangent, flipped(kernel_b)) * silu_slope(pre_act)).astype(jnp.bfloat16)
    input_grad = (cotangent.astype(jnp.float32) + cube_conv(grad_pre, flipped(kernel_a)) * silu_slope(float_in)).astype(jnp.bfloat16)
    chosen = jnp.take(generated, listed, axis=0)
    plane_all = plane_map(chosen, plane_kernel, plane_head)
    groups = N_TM // LISTED
    quarter = RD // groups
    plane_scores = plane_all.reshape(LISTED, N_SPACE, groups, quarter, W).transpose(0, 2, 1, 3, 4).reshape(N_TM, N_SPACE, quarter, W)
    pooled = pool_pairs(generated)
    rimmed = jnp.pad(pooled, ((1, 1), (0, 0), (0, 0), (0, 0)))
    time_mean = jnp.mean(jax.nn.silu(time_conv(rimmed, time_kernel)), axis=0)
    time_scores = time_head_map(time_mean, time_mixer, time_head).reshape(N_SPACE, HPT, WP)
    return generated, input_grad, plane_scores, time_scores
```

```python
import functools

import jax
import jax.numpy as jnp
from jax import lax
from jax.experimental import pallas as pl
from jax.experimental.pallas import tpu as pltpu
from jax.sharding import PartitionSpec as P

LISTED = 8
F32 = jnp.float32
BF16 = jnp.bfloat16
MIB = 1 << 20


def logistic(x):
    return 0.5 + 0.5 * jnp.tanh(0.5 * x)


def shifted(x, lane):
    width = x.shape[1]
    left = jnp.where(lane == 0, jnp.zeros_like(x), pltpu.roll(x, 1, 1))
    right = jnp.where(lane == width - 1, jnp.zeros_like(x), pltpu.roll(x, width - 1, 1))
    return left, x, right


def taps(x, silu_in):
    x = x.astype(F32)
    lane = lax.broadcasted_iota(jnp.int32, x.shape, 1)
    if silu_in:
        x = x * logistic(x)
    return [t.astype(BF16) for t in shifted(x, lane)]


def conv_rows(load, weight_ref, rows, emit, silu_in=False, frames=3):
    def pair(p):
        sides = []
        for j in range(2):
            parts = []
            for a in range(frames):
                parts += taps(load(a, 2 * p + j), silu_in)
            sides.append(jnp.concatenate(parts, axis=0))
        y = jnp.dot(weight_ref[...], jnp.concatenate(sides, axis=1), preferred_element_type=F32)
        n, w = y.shape[0] // 3, y.shape[1] // 2
        return [[y[b * n : (b + 1) * n, j * w : (j + 1) * w] for j in range(2)] for b in range(3)]

    y = pair(0)
    carry = (y[0][0] + y[1][1], y[0][1])

    def step(p, carry):
        y = pair(p)
        emit(2 * p - 2, carry[0] + y[2][0])
        emit(2 * p - 1, carry[1] + y[1][0] + y[2][1])
        return (y[0][0] + y[1][1], y[0][1])

    lax.fori_loop(1, rows // 2, step, carry)


def copies(pairs, sems):
    todo = [pltpu.make_async_copy(s, d, sems.at[i]) for i, (s, d) in enumerate(pairs)]
    for t in todo:
        t.start()
    for t in todo:
        t.wait()


def row_mask(first, r, limit):
    g = first + r
    return jnp.where((g >= 0) & (g < limit), 1.0, 0.0).astype(F32)


def first_kernel(pos, w, own, prev, nxt, up, dn, cor_p, cor_n, inner, slope, vol, sems):
    n = own.shape[0]
    copies(
        [
            (prev, vol.at[0, pl.ds(3, n)]),
            (own, vol.at[1, pl.ds(3, n)]),
            (nxt, vol.at[2, pl.ds(3, n)]),
            (up.at[pl.ds(0, 3)], vol.at[1, pl.ds(0, 3)]),
            (dn.at[pl.ds(0, 3)], vol.at[1, pl.ds(n + 3, 3)]),
            (cor_p.at[pl.ds(0, 3)], vol.at[0, pl.ds(0, 3)]),
            (cor_p.at[pl.ds(5, 3)], vol.at[0, pl.ds(n + 3, 3)]),
            (cor_n.at[pl.ds(0, 3)], vol.at[2, pl.ds(0, 3)]),
            (cor_n.at[pl.ds(5, 3)], vol.at[2, pl.ds(n + 3, 3)]),
        ],
        sems,
    )

    def emit(r, pre):
        s = logistic(pre)
        act = pre * s
        inner[r] = (act * row_mask(pos[0] - 2, r, pos[1])).astype(BF16)
        slope[r] = (s + act * (1.0 - s)).astype(BF16)

    conv_rows(lambda a, i: vol[a, i], w, n + 6, emit, silu_in=True)


def grad_kernel(pos, w, slope, own, prev, nxt, up, dn, cor_p, cor_n, grad, vol, sems):
    n = own.shape[0]
    copies(
        [
            (prev, vol.at[0, pl.ds(2, n)]),
            (own, vol.at[1, pl.ds(2, n)]),
            (nxt, vol.at[2, pl.ds(2, n)]),
            (up.at[pl.ds(3, 2)], vol.at[1, pl.ds(0, 2)]),
            (dn.at[pl.ds(3, 2)], vol.at[1, pl.ds(n + 2, 2)]),
            (cor_p.at[pl.ds(3, 2)], vol.at[0, pl.ds(0, 2)]),
            (cor_p.at[pl.ds(8, 2)], vol.at[0, pl.ds(n + 2, 2)]),
            (cor_n.at[pl.ds(3, 2)], vol.at[2, pl.ds(0, 2)]),
            (cor_n.at[pl.ds(8, 2)], vol.at[2, pl.ds(n + 2, 2)]),
        ],
        sems,
    )

    def emit(r, value):
        out = value * slope[r + 1].astype(F32)
        grad[r] = (out * row_mask(pos[0] - 1, r, pos[1])).astype(BF16)

    conv_rows(lambda a, i: vol[a, i], w, n + 4, emit)


def video_kernel(
    pos, listed, w, wp, head, pool, base, up, dn, own, prev, nxt, video, send, rim, sums, sems
):
    n = base.shape[0]
    copies(
        [
            (base, rim.at[pl.ds(1, n)]),
            (up.at[pl.ds(2, 1)], rim.at[pl.ds(0, 1)]),
            (dn.at[pl.ds(0, 1)], rim.at[pl.ds(n + 1, 1)]),
        ],
        sems,
    )
    vol = (prev, own, nxt)

    def emit(r, value):
        out = (rim[r].astype(F32) + value) * row_mask(pos[0] - 1, r, pos[1])
        rim[r] = out.astype(BF16)

    conv_rows(lambda a, i: vol[a][i], w, n + 4, emit)

    def emit_plane(r, value):
        act = value * logistic(value) * head[...]
        sums[pl.ds(r, 1)] = jnp.sum(act, axis=0, keepdims=True)

    conv_rows(lambda a, i: rim[i], wp, n + 2, emit_plane, frames=1)

    def pool_row(i, _):
        a, b = rim[2 * i + 1], rim[2 * i + 2]
        video[2 * i] = a
        video[2 * i + 1] = b
        both = jnp.dot(jnp.concatenate([a, b], axis=1), pool[...], preferred_element_type=F32)
        half = both.shape[0] // 2
        lane = lax.broadcasted_iota(jnp.int32, (half, both.shape[1]), 1)
        packed = jnp.where(lane < both.shape[1] // 2, both[:half], both[half:])
        send[i, pl.ds(0, half)] = packed.astype(BF16)
        return 0

    lax.fori_loop(0, n // 2, pool_row, 0)

    dests = send.shape[0]
    groups = dests // LISTED
    quarter = n // groups
    base_row = send.shape[1] - quarter
    for k in range(LISTED):
        hit = jnp.where(listed[k] == pos[2], 1.0, 0.0).astype(F32)
        for q in range(groups):
            send[k * groups + q, pl.ds(base_row, quarter)] = (
                sums[q * quarter : (q + 1) * quarter] * hit
            ).astype(BF16)


def input_grad_kernel(w, cot, vin, own, prev, nxt, out):
    n = cot.shape[0]
    vol = (prev, own, nxt)

    def emit(r, value):
        x = vin[r].astype(F32)
        s = logistic(x)
        out[r] = (cot[r].astype(F32) + value * (s * (1.0 + x * (1.0 - s)))).astype(BF16)

    conv_rows(lambda a, i: vol[a][i], w, n + 2, emit)


def time_kernel_body(pos, listed, wt, mixer, head, recv, plane, score, total):
    frames = recv.shape[0]
    half, width = wt.shape[1] // 3, recv.shape[2]
    units = wt.shape[0] // 2
    plane[...] = recv[listed[pos[2] // (frames // LISTED)], pl.ds(half, plane.shape[0])].astype(F32)
    total[...] = jnp.zeros_like(total)
    lane = lax.broadcasted_iota(jnp.int32, (units, width), 1)

    def piece(t):
        ok = jnp.where((t >= 0) & (t < frames), 1.0, 0.0).astype(BF16)
        return recv[jnp.clip(t, 0, frames - 1), pl.ds(0, half)] * ok

    def step(i, _):
        f = [piece(2 * i + d) for d in (-1, 0, 1, 2)]
        rhs = jnp.concatenate(
            [jnp.concatenate(f[:3], axis=0), jnp.concatenate(f[1:], axis=0)], axis=1
        )
        y = jnp.dot(wt[...], rhs, preferred_element_type=F32)
        a, b = y[:, :width], y[:, width:]
        left = a[:units] + pltpu.roll(a[units:], width // 2, 1)
        right = pltpu.roll(b[:units], width // 2, 1) + b[units:]
        q = jnp.where(lane < width // 2, left, right)
        total[...] += q * logistic(q)
        return 0

    lax.fori_loop(0, frames // 2, step, 0)
    both = total[...]
    mean = (both + pltpu.roll(both, width // 2, 1)) * (1.0 / frames)
    mixed = jnp.zeros_like(mean)
    rest = mean
    for _ in range(3):
        top = rest.astype(BF16)
        mixed = mixed + jnp.dot(mixer[...], top, preferred_element_type=F32)
        rest = rest - top.astype(F32)
    act = mixed * logistic(mixed) * head[...]
    score[...] = jnp.sum(act, axis=0, keepdims=True)[:, : width // 2]


VMEM = pl.BlockSpec(memory_space=pltpu.VMEM)
SMEM = pl.BlockSpec(memory_space=pltpu.SMEM)
ANY = pl.BlockSpec(memory_space=pl.ANY)


def call(body, outs, in_specs, scratch, flops, nbytes, limit=40):
    return pl.pallas_call(
        body,
        out_shape=outs,
        in_specs=in_specs,
        out_specs=jax.tree.map(lambda _: VMEM, outs),
        scratch_shapes=scratch,
        compiler_params=pltpu.CompilerParams(vmem_limit_bytes=limit * MIB),
        cost_estimate=pl.CostEstimate(flops=flops, bytes_accessed=nbytes, transcendentals=0),
    )


def stacked(kernel):
    a, b, e, c, o = kernel.shape
    return jnp.transpose(kernel, (1, 4, 0, 2, 3)).reshape(b * o, a * e * c)


def flipped(kernel):
    return jnp.swapaxes(kernel[::-1, ::-1, ::-1], 3, 4)


def shards(
    video_in,
    cotangent,
    kernel_a,
    kernel_b,
    plane_kernel,
    plane_head,
    time_kernel,
    time_mixer,
    time_head,
    listed,
):
    v, c = video_in[0], cotangent[0]
    n, ch, width = v.shape
    tm, sp = lax.axis_size("tm"), lax.axis_size("space")
    up_tm = [(i, i + 1) for i in range(tm - 1)]
    dn_tm = [(j, i) for i, j in up_tm]
    up_sp = [(i, i + 1) for i in range(sp - 1)]
    dn_sp = [(j, i) for i, j in up_sp]
    me = lax.axis_index("tm")
    pos = jnp.stack([lax.axis_index("space") * n, sp * n, me]).astype(jnp.int32)

    def both(x):
        return lax.ppermute(x, "tm", up_tm), lax.ppermute(x, "tm", dn_tm)

    up = lax.ppermute(jnp.concatenate([v[n - 3 :], c[n - 2 :]]), "space", up_sp)
    dn = lax.ppermute(jnp.concatenate([v[:3], c[:2]]), "space", dn_sp)
    v_p, v_n = both(v)
    cor_p, cor_n = both(jnp.concatenate([up, dn]))
    c_p, c_n = both(c)

    def rows(r, dtype=BF16):
        return jax.ShapeDtypeStruct((r, ch, width), dtype)

    def volume(r):
        return [pltpu.VMEM((3, r, ch, width), BF16), pltpu.SemaphoreType.DMA((9,))]

    flops = 2 * 27 * ch * ch * width * n
    wa, wb = stacked(kernel_a), stacked(kernel_b)
    wbt, wat = stacked(flipped(kernel_b)), stacked(flipped(kernel_a))
    inner, slope = call(
        first_kernel, (rows(n + 4), rows(n + 4)), [SMEM, VMEM] + [ANY] * 7, volume(n + 6), flops, 6 * MIB
    )(pos, wa, v, v_p, v_n, up, dn, cor_p, cor_n)
    in_p, in_n = both(inner)
    grad = call(
        grad_kernel, rows(n + 2), [SMEM, VMEM, VMEM] + [ANY] * 7, volume(n + 4), flops, 6 * MIB
    )(pos, wbt, slope, c, c_p, c_n, up, dn, cor_p, cor_n)
    gr_p, gr_n = both(grad)

    wp = stacked(plane_kernel[None])
    spread = lambda h: jnp.broadcast_to(h.astype(F32)[:, None], (ch, width))
    idx = jnp.arange(2 * width)[:, None] % width // 2
    pool = jnp.where(idx == jnp.arange(width)[None, :] % (width // 2), 0.25, 0.0).astype(BF16)
    quarter = n // (tm // LISTED)
    video, send = call(
        video_kernel,
        (rows(n), jax.ShapeDtypeStruct((tm, ch // 2 + quarter, width), BF16)),
        [SMEM, SMEM, VMEM, VMEM, VMEM, VMEM, ANY, ANY, ANY, VMEM, VMEM, VMEM],
        [
            pltpu.VMEM((n + 2, ch, width), BF16),
            pltpu.VMEM((n, width), F32),
            pltpu.SemaphoreType.DMA((3,)),
        ],
        flops * 4 // 3,
        6 * MIB,
    )(pos, listed, wb, wp, spread(plane_head), pool, v, up, dn, inner, in_p, in_n)
    recv = lax.all_to_all(send, "tm", split_axis=0, concat_axis=0, tiled=True)
    input_grad = call(input_grad_kernel, rows(n), [VMEM] * 6, [], flops, 6 * MIB)(
        wat, c, v, grad, gr_p, gr_n
    )
    wt = jnp.transpose(time_kernel.reshape(3, 2, ch // 2, ch), (1, 3, 0, 2)).reshape(2 * ch, 3 * ch // 2)
    plane_scores, time_scores = call(
        time_kernel_body,
        (jax.ShapeDtypeStruct((quarter, width), F32), jax.ShapeDtypeStruct((1, width // 2), F32)),
        [SMEM, SMEM, VMEM, VMEM, VMEM, VMEM],
        [pltpu.VMEM((ch, width), F32)],
        flops // 20,
        MIB,
    )(pos, listed, wt, time_mixer.T, spread(time_head), recv)
    return (video[None], input_grad[None], plane_scores[None, None], time_scores[None])


def solution(mesh):
    return jax.shard_map(
        shards,
        mesh=mesh,
        in_specs=(P("tm", "space", None, None), P("tm", "space", None, None)) + (P(),) * 8,
        out_specs=(
            P("tm", "space", None, None),
            P("tm", "space", None, None),
            P("tm", "space", None, None),
            P("space", "tm", None),
        ),
        check_vma=False,
    )
```

```python
import functools

import jax
import jax.numpy as jnp
from jax import lax
from jax.experimental import pallas as pl
from jax.experimental.pallas import tpu as pltpu
from jax.sharding import PartitionSpec as P

LISTED = 8
F32 = jnp.float32
BF16 = jnp.bfloat16
MIB = 1 << 20
UNROLL = 16


def logistic(x):
    return 0.5 + 0.5 * jnp.tanh(0.5 * x)


def shifted(x, lane):
    width = x.shape[1]
    left = jnp.where(lane == 0, jnp.zeros_like(x), pltpu.roll(x, 1, 1))
    right = jnp.where(lane == width - 1, jnp.zeros_like(x), pltpu.roll(x, width - 1, 1))
    return left, x, right


def taps(x, silu_in):
    x = x.astype(F32)
    lane = lax.broadcasted_iota(jnp.int32, x.shape, 1)
    if silu_in:
        x = x * logistic(x)
    return [t.astype(BF16) for t in shifted(x, lane)]


def conv_rows(load, weight_ref, rows, emit, silu_in=False, frames=3, unroll=UNROLL):
    def pair(p):
        sides = []
        for j in range(2):
            parts = []
            for a in range(frames):
                parts += taps(load(a, 2 * p + j), silu_in)
            sides.append(jnp.concatenate(parts, axis=0))
        y = jnp.dot(weight_ref[...], jnp.concatenate(sides, axis=1), preferred_element_type=F32)
        n, w = y.shape[0] // 3, y.shape[1] // 2
        return [[y[b * n : (b + 1) * n, j * w : (j + 1) * w] for j in range(2)] for b in range(3)]

    y = pair(0)
    carry = (y[0][0] + y[1][1], y[0][1])

    def step(p, carry):
        y = pair(p)
        emit(2 * p - 2, carry[0] + y[2][0])
        emit(2 * p - 1, carry[1] + y[1][0] + y[2][1])
        return (y[0][0] + y[1][1], y[0][1])

    lax.fori_loop(1, rows // 2, step, carry, unroll=unroll)


def copies(pairs, sems):
    todo = [pltpu.make_async_copy(s, d, sems.at[i]) for i, (s, d) in enumerate(pairs)]
    for t in todo:
        t.start()
    for t in todo:
        t.wait()


def row_mask(first, r, limit):
    g = first + r
    return jnp.where((g >= 0) & (g < limit), 1.0, 0.0).astype(F32)


def first_kernel(pos, w, own, prev, nxt, up, dn, cor_p, cor_n, inner, slope, vol, sems):
    n = own.shape[0]
    copies(
        [
            (prev, vol.at[0, pl.ds(3, n)]),
            (own, vol.at[1, pl.ds(3, n)]),
            (nxt, vol.at[2, pl.ds(3, n)]),
            (up.at[pl.ds(0, 3)], vol.at[1, pl.ds(0, 3)]),
            (dn.at[pl.ds(0, 3)], vol.at[1, pl.ds(n + 3, 3)]),
            (cor_p.at[pl.ds(0, 3)], vol.at[0, pl.ds(0, 3)]),
            (cor_p.at[pl.ds(3, 3)], vol.at[0, pl.ds(n + 3, 3)]),
            (cor_n.at[pl.ds(0, 3)], vol.at[2, pl.ds(0, 3)]),
            (cor_n.at[pl.ds(3, 3)], vol.at[2, pl.ds(n + 3, 3)]),
        ],
        sems,
    )

    def emit(r, pre):
        s = logistic(pre)
        act = pre * s
        inner[r] = (act * row_mask(pos[0] - 2, r, pos[1])).astype(BF16)
        slope[r] = (s + act * (1.0 - s)).astype(BF16)

    conv_rows(lambda a, i: vol[a, i], w, n + 6, emit, silu_in=True)


def grad_kernel(pos, w, slope, own, prev, nxt, grad):
    n = own.shape[0] - 4
    vol = (prev, own, nxt)

    def emit(r, value):
        out = value * slope[r + 1].astype(F32)
        grad[r] = (out * row_mask(pos[0] - 1, r, pos[1])).astype(BF16)

    conv_rows(lambda a, i: vol[a][i], w, n + 4, emit)


def video_kernel(
    pos, listed, w, wp, head, pool, base, up, dn, own, prev, nxt, video, send, rim, sums, sems
):
    n = base.shape[0]
    copies(
        [
            (base, rim.at[pl.ds(1, n)]),
            (up.at[pl.ds(2, 1)], rim.at[pl.ds(0, 1)]),
            (dn.at[pl.ds(0, 1)], rim.at[pl.ds(n + 1, 1)]),
        ],
        sems,
    )
    vol = (prev, own, nxt)

    def emit(r, value):
        out = (rim[r].astype(F32) + value) * row_mask(pos[0] - 1, r, pos[1])
        rim[r] = out.astype(BF16)

    conv_rows(lambda a, i: vol[a][i], w, n + 4, emit)

    def emit_plane(r, value):
        act = value * logistic(value) * head[...]
        sums[pl.ds(r, 1)] = jnp.sum(act, axis=0, keepdims=True)

    conv_rows(lambda a, i: rim[i], wp, n + 2, emit_plane, frames=1)

    def pool_row(i, _):
        a, b = rim[2 * i + 1], rim[2 * i + 2]
        video[2 * i] = a
        video[2 * i + 1] = b
        both = jnp.dot(jnp.concatenate([a, b], axis=1), pool[...], preferred_element_type=F32)
        half = both.shape[0] // 2
        lane = lax.broadcasted_iota(jnp.int32, (half, both.shape[1]), 1)
        packed = jnp.where(lane < both.shape[1] // 2, both[:half], both[half:])
        send[i, pl.ds(0, half)] = packed.astype(BF16)
        return 0

    lax.fori_loop(0, n // 2, pool_row, 0, unroll=8)

    dests = send.shape[0]
    groups = dests // LISTED
    quarter = n // groups
    base_row = send.shape[1] - quarter
    for k in range(LISTED):
        hit = jnp.where(listed[k] == pos[2], 1.0, 0.0).astype(F32)
        for q in range(groups):
            send[k * groups + q, pl.ds(base_row, quarter)] = (
                sums[q * quarter : (q + 1) * quarter] * hit
            ).astype(BF16)


def input_grad_kernel(w, cot, vin, own, prev, nxt, out):
    n = cot.shape[0]
    vol = (prev, own, nxt)

    def emit(r, value):
        x = vin[r].astype(F32)
        s = logistic(x)
        out[r] = (cot[r].astype(F32) + value * (s * (1.0 + x * (1.0 - s)))).astype(BF16)

    conv_rows(lambda a, i: vol[a][i], w, n + 2, emit)


def time_kernel_body(pos, listed, wt, mixer, head, recv, plane, score, total):
    frames = recv.shape[0]
    half, width = wt.shape[1] // 3, recv.shape[2]
    units = wt.shape[0] // 2
    plane[...] = recv[listed[pos[2] // (frames // LISTED)], pl.ds(half, plane.shape[0])].astype(F32)
    total[...] = jnp.zeros_like(total)
    lane = lax.broadcasted_iota(jnp.int32, (units, width), 1)

    def piece(t):
        ok = jnp.where((t >= 0) & (t < frames), 1.0, 0.0).astype(BF16)
        return recv[jnp.clip(t, 0, frames - 1), pl.ds(0, half)] * ok

    def step(i, _):
        f = [piece(2 * i + d) for d in (-1, 0, 1, 2)]
        rhs = jnp.concatenate(
            [jnp.concatenate(f[:3], axis=0), jnp.concatenate(f[1:], axis=0)], axis=1
        )
        y = jnp.dot(wt[...], rhs, preferred_element_type=F32)
        a, b = y[:, :width], y[:, width:]
        left = a[:units] + pltpu.roll(a[units:], width // 2, 1)
        right = pltpu.roll(b[:units], width // 2, 1) + b[units:]
        q = jnp.where(lane < width // 2, left, right)
        total[...] += q * logistic(q)
        return 0

    lax.fori_loop(0, frames // 2, step, 0, unroll=8)
    both = total[...]
    mean = (both + pltpu.roll(both, width // 2, 1)) * (1.0 / frames)
    mixed = jnp.zeros_like(mean)
    rest = mean
    for _ in range(3):
        top = rest.astype(BF16)
        mixed = mixed + jnp.dot(mixer[...], top, preferred_element_type=F32)
        rest = rest - top.astype(F32)
    act = mixed * logistic(mixed) * head[...]
    score[...] = jnp.sum(act, axis=0, keepdims=True)[:, : width // 2]


VMEM = pl.BlockSpec(memory_space=pltpu.VMEM)
SMEM = pl.BlockSpec(memory_space=pltpu.SMEM)
ANY = pl.BlockSpec(memory_space=pl.ANY)


def call(body, outs, in_specs, scratch, flops, nbytes, limit=40):
    return pl.pallas_call(
        body,
        out_shape=outs,
        in_specs=in_specs,
        out_specs=jax.tree.map(lambda _: VMEM, outs),
        scratch_shapes=scratch,
        compiler_params=pltpu.CompilerParams(vmem_limit_bytes=limit * MIB),
        cost_estimate=pl.CostEstimate(flops=flops, bytes_accessed=nbytes, transcendentals=0),
    )


def stacked(kernel):
    a, b, e, c, o = kernel.shape
    return jnp.transpose(kernel, (1, 4, 0, 2, 3)).reshape(b * o, a * e * c)


def flipped(kernel):
    return jnp.swapaxes(kernel[::-1, ::-1, ::-1], 3, 4)


def shards(
    video_in,
    cotangent,
    kernel_a,
    kernel_b,
    plane_kernel,
    plane_head,
    time_kernel,
    time_mixer,
    time_head,
    listed,
):
    v, c = video_in[0], cotangent[0]
    n, ch, width = v.shape
    tm, sp = lax.axis_size("tm"), lax.axis_size("space")
    up_tm = [(i, i + 1) for i in range(tm - 1)]
    dn_tm = [(j, i) for i, j in up_tm]
    up_sp = [(i, i + 1) for i in range(sp - 1)]
    dn_sp = [(j, i) for i, j in up_sp]
    me = lax.axis_index("tm")
    pos = jnp.stack([lax.axis_index("space") * n, sp * n, me]).astype(jnp.int32)

    def both(x):
        return lax.ppermute(x, "tm", up_tm), lax.ppermute(x, "tm", dn_tm)

    up = lax.ppermute(jnp.concatenate([v[n - 3 :], c[n - 2 :]]), "space", up_sp)
    dn = lax.ppermute(jnp.concatenate([v[:3], c[:2]]), "space", dn_sp)
    v_p, v_n = both(v)
    cor_p, cor_n = both(jnp.concatenate([up[:3], dn[:3]]))
    wa, wb = stacked(kernel_a), stacked(kernel_b)
    wbt, wat = stacked(flipped(kernel_b)), stacked(flipped(kernel_a))
    c_own = jnp.concatenate([up[3:], c, dn[3:]])
    c_own, cor_p, cor_n, wa, wb, wbt, wat = lax.optimization_barrier(
        (c_own, cor_p, cor_n, wa, wb, wbt, wat)
    )
    c_p, c_n = both(c_own)

    def rows(r, dtype=BF16):
        return jax.ShapeDtypeStruct((r, ch, width), dtype)

    def volume(r):
        return [pltpu.VMEM((3, r, ch, width), BF16), pltpu.SemaphoreType.DMA((9,))]

    flops = 2 * 27 * ch * ch * width * n
    inner, slope = call(
        first_kernel, (rows(n + 4), rows(n + 4)), [SMEM, VMEM] + [ANY] * 7, volume(n + 6), flops, 6 * MIB
    )(pos, wa, v, v_p, v_n, up, dn, cor_p, cor_n)
    in_p, in_n = both(inner)
    grad = call(
        grad_kernel, rows(n + 2), [SMEM] + [VMEM] * 5, [], flops, 6 * MIB
    )(pos, wbt, slope, c_own, c_p, c_n)
    gr_p, gr_n = both(grad)

    wp = stacked(plane_kernel[None])
    spread = lambda h: jnp.broadcast_to(h.astype(F32)[:, None], (ch, width))
    idx = jnp.arange(2 * width)[:, None] % width // 2
    pool = jnp.where(idx == jnp.arange(width)[None, :] % (width // 2), 0.25, 0.0).astype(BF16)
    quarter = n // (tm // LISTED)
    video, send = call(
        video_kernel,
        (rows(n), jax.ShapeDtypeStruct((tm, ch // 2 + quarter, width), BF16)),
        [SMEM, SMEM, VMEM, VMEM, VMEM, VMEM, ANY, ANY, ANY, VMEM, VMEM, VMEM],
        [
            pltpu.VMEM((n + 2, ch, width), BF16),
            pltpu.VMEM((n, width), F32),
            pltpu.SemaphoreType.DMA((3,)),
        ],
        flops * 4 // 3,
        6 * MIB,
    )(pos, listed, wb, wp, spread(plane_head), pool, v, up, dn, inner, in_p, in_n)
    recv = lax.all_to_all(send, "tm", split_axis=0, concat_axis=0, tiled=True)
    input_grad = call(input_grad_kernel, rows(n), [VMEM] * 6, [], flops, 6 * MIB)(
        wat, c, v, grad, gr_p, gr_n
    )
    wt = jnp.transpose(time_kernel.reshape(3, 2, ch // 2, ch), (1, 3, 0, 2)).reshape(2 * ch, 3 * ch // 2)
    plane_scores, time_scores = call(
        time_kernel_body,
        (jax.ShapeDtypeStruct((quarter, width), F32), jax.ShapeDtypeStruct((1, width // 2), F32)),
        [SMEM, SMEM, VMEM, VMEM, VMEM, VMEM],
        [pltpu.VMEM((ch, width), F32)],
        flops // 20,
        MIB,
    )(pos, listed, wt, time_mixer.T, spread(time_head), recv)
    return (video[None], input_grad[None], plane_scores[None, None], time_scores[None])


def solution(mesh):
    return jax.shard_map(
        shards,
        mesh=mesh,
        in_specs=(P("tm", "space", None, None), P("tm", "space", None, None)) + (P(),) * 8,
        out_specs=(
            P("tm", "space", None, None),
            P("tm", "space", None, None),
            P("tm", "space", None, None),
            P("space", "tm", None),
        ),
        check_vma=False,
    )
```

```python
import functools

import jax
import jax.numpy as jnp
from jax import lax
from jax.experimental import pallas as pl
from jax.experimental.pallas import tpu as pltpu
from jax.sharding import PartitionSpec as P

LISTED = 8
F32 = jnp.float32
BF16 = jnp.bfloat16
MIB = 1 << 20
UNROLL = 16


def logistic(x):
    return 0.5 + 0.5 * jnp.tanh(0.5 * x)


def shifted(x, lane):
    width = x.shape[1]
    left = jnp.where(lane == 0, jnp.zeros_like(x), pltpu.roll(x, 1, 1))
    right = jnp.where(lane == width - 1, jnp.zeros_like(x), pltpu.roll(x, width - 1, 1))
    return left, x, right


def taps(x, silu_in):
    x = x.astype(F32)
    lane = lax.broadcasted_iota(jnp.int32, x.shape, 1)
    if silu_in:
        x = x * logistic(x)
    return [t.astype(BF16) for t in shifted(x, lane)]


def conv_rows(load, weight_ref, rows, emit, silu_in=False, frames=3, unroll=UNROLL):
    def pair(p):
        sides = []
        for j in range(2):
            parts = []
            for a in range(frames):
                parts += taps(load(a, 2 * p + j), silu_in)
            sides.append(jnp.concatenate(parts, axis=0))
        y = jnp.dot(weight_ref[...], jnp.concatenate(sides, axis=1), preferred_element_type=F32)
        n, w = y.shape[0] // 3, y.shape[1] // 2
        return [[y[b * n : (b + 1) * n, j * w : (j + 1) * w] for j in range(2)] for b in range(3)]

    y = pair(0)
    carry = (y[0][0] + y[1][1], y[0][1])

    def step(p, carry):
        y = pair(p)
        emit(2 * p - 2, carry[0] + y[2][0])
        emit(2 * p - 1, carry[1] + y[1][0] + y[2][1])
        return (y[0][0] + y[1][1], y[0][1])

    lax.fori_loop(1, rows // 2, step, carry, unroll=unroll)


def row_mask(first, r, limit):
    g = first + r
    return jnp.where((g >= 0) & (g < limit), 1.0, 0.0).astype(F32)


def first_kernel(pos, w, own, prev, nxt, inner, slope):
    n = own.shape[0] - 6
    vol = (prev, own, nxt)

    def emit(r, pre):
        s = logistic(pre)
        act = pre * s
        inner[r] = (act * row_mask(pos[0] - 2, r, pos[1])).astype(BF16)
        slope[r] = (s + act * (1.0 - s)).astype(BF16)

    conv_rows(lambda a, i: vol[a][i], w, n + 6, emit, silu_in=True)


def grad_kernel(pos, w, slope, own, prev, nxt, grad):
    n = own.shape[0] - 4
    vol = (prev, own, nxt)

    def emit(r, value):
        out = value * slope[r + 1].astype(F32)
        grad[r] = (out * row_mask(pos[0] - 1, r, pos[1])).astype(BF16)

    conv_rows(lambda a, i: vol[a][i], w, n + 4, emit)


def video_kernel(pos, listed, w, wp, head, pool, base, own, prev, nxt, video, send, rim, sums):
    n = base.shape[0] - 6
    vol = (prev, own, nxt)

    def emit(r, value):
        out = (base[r + 2].astype(F32) + value) * row_mask(pos[0] - 1, r, pos[1])
        rim[r] = out.astype(BF16)

    conv_rows(lambda a, i: vol[a][i], w, n + 4, emit)

    def emit_plane(r, value):
        act = value * logistic(value) * head[...]
        sums[pl.ds(r, 1)] = jnp.sum(act, axis=0, keepdims=True)

    conv_rows(lambda a, i: rim[i], wp, n + 2, emit_plane, frames=1)

    def pool_row(i, _):
        a, b = rim[2 * i + 1], rim[2 * i + 2]
        video[2 * i] = a
        video[2 * i + 1] = b
        both = jnp.dot(jnp.concatenate([a, b], axis=1), pool[...], preferred_element_type=F32)
        half = both.shape[0] // 2
        lane = lax.broadcasted_iota(jnp.int32, (half, both.shape[1]), 1)
        packed = jnp.where(lane < both.shape[1] // 2, both[:half], both[half:])
        send[i, pl.ds(0, half)] = packed.astype(BF16)
        return 0

    lax.fori_loop(0, n // 2, pool_row, 0, unroll=8)

    dests = send.shape[0]
    groups = dests // LISTED
    quarter = n // groups
    base_row = send.shape[1] - quarter
    for k in range(LISTED):
        hit = jnp.where(listed[k] == pos[2], 1.0, 0.0).astype(F32)
        for q in range(groups):
            send[k * groups + q, pl.ds(base_row, quarter)] = (
                sums[q * quarter : (q + 1) * quarter] * hit
            ).astype(BF16)


def input_grad_kernel(w, cot, vin, own, prev, nxt, out):
    n = cot.shape[0]
    vol = (prev, own, nxt)

    def emit(r, value):
        x = vin[r].astype(F32)
        s = logistic(x)
        out[r] = (cot[r].astype(F32) + value * (s * (1.0 + x * (1.0 - s)))).astype(BF16)

    conv_rows(lambda a, i: vol[a][i], w, n + 2, emit)


def time_kernel_body(pos, listed, wt, mixer, head, recv, plane, score, total):
    frames = recv.shape[0]
    half, width = wt.shape[1] // 3, recv.shape[2]
    units = wt.shape[0] // 2
    plane[...] = recv[listed[pos[2] // (frames // LISTED)], pl.ds(half, plane.shape[0])].astype(F32)
    total[...] = jnp.zeros_like(total)
    lane = lax.broadcasted_iota(jnp.int32, (units, width), 1)

    def piece(t):
        ok = jnp.where((t >= 0) & (t < frames), 1.0, 0.0).astype(BF16)
        return recv[jnp.clip(t, 0, frames - 1), pl.ds(0, half)] * ok

    def step(i, _):
        f = [piece(2 * i + d) for d in (-1, 0, 1, 2)]
        rhs = jnp.concatenate(
            [jnp.concatenate(f[:3], axis=0), jnp.concatenate(f[1:], axis=0)], axis=1
        )
        y = jnp.dot(wt[...], rhs, preferred_element_type=F32)
        a, b = y[:, :width], y[:, width:]
        left = a[:units] + pltpu.roll(a[units:], width // 2, 1)
        right = pltpu.roll(b[:units], width // 2, 1) + b[units:]
        q = jnp.where(lane < width // 2, left, right)
        total[...] += q * logistic(q)
        return 0

    lax.fori_loop(0, frames // 2, step, 0, unroll=8)
    both = total[...]
    mean = (both + pltpu.roll(both, width // 2, 1)) * (1.0 / frames)
    mixed = jnp.zeros_like(mean)
    rest = mean
    for _ in range(3):
        top = rest.astype(BF16)
        mixed = mixed + jnp.dot(mixer[...], top, preferred_element_type=F32)
        rest = rest - top.astype(F32)
    act = mixed * logistic(mixed) * head[...]
    score[...] = jnp.sum(act, axis=0, keepdims=True)[:, : width // 2]


VMEM = pl.BlockSpec(memory_space=pltpu.VMEM)
SMEM = pl.BlockSpec(memory_space=pltpu.SMEM)


def call(body, outs, in_specs, scratch, flops, nbytes, limit=40):
    return pl.pallas_call(
        body,
        out_shape=outs,
        in_specs=in_specs,
        out_specs=jax.tree.map(lambda _: VMEM, outs),
        scratch_shapes=scratch,
        compiler_params=pltpu.CompilerParams(vmem_limit_bytes=limit * MIB),
        cost_estimate=pl.CostEstimate(flops=flops, bytes_accessed=nbytes, transcendentals=0),
    )


def stacked(kernel):
    a, b, e, c, o = kernel.shape
    return jnp.transpose(kernel, (1, 4, 0, 2, 3)).reshape(b * o, a * e * c)


def flipped(kernel):
    return jnp.swapaxes(kernel[::-1, ::-1, ::-1], 3, 4)


def shards(
    video_in,
    cotangent,
    kernel_a,
    kernel_b,
    plane_kernel,
    plane_head,
    time_kernel,
    time_mixer,
    time_head,
    listed,
):
    v, c = video_in[0], cotangent[0]
    n, ch, width = v.shape
    tm, sp = lax.axis_size("tm"), lax.axis_size("space")
    up_tm = [(i, i + 1) for i in range(tm - 1)]
    dn_tm = [(j, i) for i, j in up_tm]
    up_sp = [(i, i + 1) for i in range(sp - 1)]
    dn_sp = [(j, i) for i, j in up_sp]
    me = lax.axis_index("tm")
    pos = jnp.stack([lax.axis_index("space") * n, sp * n, me]).astype(jnp.int32)

    def both(x):
        return lax.ppermute(x, "tm", up_tm), lax.ppermute(x, "tm", dn_tm)

    up = lax.ppermute(jnp.concatenate([v[n - 3 :], c[n - 2 :]]), "space", up_sp)
    dn = lax.ppermute(jnp.concatenate([v[:3], c[:2]]), "space", dn_sp)
    v_own = jnp.concatenate([up[:3], v, dn[:3]])
    c_own = jnp.concatenate([up[3:], c, dn[3:]])
    v_p, v_n = both(v_own)
    c_p, c_n = both(c_own)
    wa, wb = stacked(kernel_a), stacked(kernel_b)
    wbt, wat = stacked(flipped(kernel_b)), stacked(flipped(kernel_a))
    wp = stacked(plane_kernel[None])
    spread = lambda h: jnp.broadcast_to(h.astype(F32)[:, None], (ch, width))
    idx = jnp.arange(2 * width)[:, None] % width // 2
    pool = jnp.where(idx == jnp.arange(width)[None, :] % (width // 2), 0.25, 0.0).astype(BF16)
    wt = jnp.transpose(time_kernel.reshape(3, 2, ch // 2, ch), (1, 3, 0, 2)).reshape(2 * ch, 3 * ch // 2)
    mixer, plane_row, time_row = time_mixer.T, spread(plane_head), spread(time_head)
    wa, wb, wbt, wat, wp, wt, mixer, plane_row, time_row, pool = lax.optimization_barrier(
        (wa, wb, wbt, wat, wp, wt, mixer, plane_row, time_row, pool)
    )

    def rows(r, dtype=BF16):
        return jax.ShapeDtypeStruct((r, ch, width), dtype)

    flops = 2 * 27 * ch * ch * width * n
    inner, slope = call(
        first_kernel, (rows(n + 4), rows(n + 4)), [SMEM] + [VMEM] * 4, [], flops, 6 * MIB
    )(pos, wa, v_own, v_p, v_n)
    in_p, in_n = both(inner)
    grad = call(
        grad_kernel, rows(n + 2), [SMEM] + [VMEM] * 5, [], flops, 6 * MIB
    )(pos, wbt, slope, c_own, c_p, c_n)
    gr_p, gr_n = both(grad)

    quarter = n // (tm // LISTED)
    video, send = call(
        video_kernel,
        (rows(n), jax.ShapeDtypeStruct((tm, ch // 2 + quarter, width), BF16)),
        [SMEM, SMEM] + [VMEM] * 8,
        [
            pltpu.VMEM((n + 2, ch, width), BF16),
            pltpu.VMEM((n, width), F32),
        ],
        flops * 4 // 3,
        6 * MIB,
    )(pos, listed, wb, wp, plane_row, pool, v_own, inner, in_p, in_n)
    recv = lax.all_to_all(send, "tm", split_axis=0, concat_axis=0, tiled=True)
    input_grad = call(input_grad_kernel, rows(n), [VMEM] * 6, [], flops, 6 * MIB)(
        wat, c, v, grad, gr_p, gr_n
    )
    plane_scores, time_scores = call(
        time_kernel_body,
        (jax.ShapeDtypeStruct((quarter, width), F32), jax.ShapeDtypeStruct((1, width // 2), F32)),
        [SMEM, SMEM, VMEM, VMEM, VMEM, VMEM],
        [pltpu.VMEM((ch, width), F32)],
        flops // 20,
        MIB,
    )(pos, listed, wt, mixer, time_row, recv)
    return (video[None], input_grad[None], plane_scores[None, None], time_scores[None])


def solution(mesh):
    return jax.shard_map(
        shards,
        mesh=mesh,
        in_specs=(P("tm", "space", None, None), P("tm", "space", None, None)) + (P(),) * 8,
        out_specs=(
            P("tm", "space", None, None),
            P("tm", "space", None, None),
            P("tm", "space", None, None),
            P("space", "tm", None),
        ),
        check_vma=False,
    )
```

```python
import functools

import jax
import jax.numpy as jnp
from jax import lax
from jax.experimental import pallas as pl
from jax.experimental.pallas import tpu as pltpu
from jax.sharding import PartitionSpec as P

LISTED = 8
F32 = jnp.float32
BF16 = jnp.bfloat16
MIB = 1 << 20


def logistic(x):
    return 0.5 + 0.5 * jnp.tanh(0.5 * x)


def shifted(x, lane):
    width = x.shape[1]
    left = jnp.where(lane == 0, jnp.zeros_like(x), pltpu.roll(x, 1, 1))
    right = jnp.where(lane == width - 1, jnp.zeros_like(x), pltpu.roll(x, width - 1, 1))
    return left, x, right


def taps(x, silu_in):
    x = x.astype(F32)
    lane = lax.broadcasted_iota(jnp.int32, x.shape, 1)
    if silu_in:
        x = x * logistic(x)
    return [t.astype(BF16) for t in shifted(x, lane)]


def conv_rows(load, weight_ref, rows, emit, silu_in=False, frames=3):
    def pair(p):
        sides = []
        for j in range(2):
            parts = []
            for a in range(frames):
                parts += taps(load(a, 2 * p + j), silu_in)
            sides.append(jnp.concatenate(parts, axis=0))
        y = jnp.dot(weight_ref[...], jnp.concatenate(sides, axis=1), preferred_element_type=F32)
        n, w = y.shape[0] // 3, y.shape[1] // 2
        return [[y[b * n : (b + 1) * n, j * w : (j + 1) * w] for j in range(2)] for b in range(3)]

    y = pair(0)
    carry = (y[0][0] + y[1][1], y[0][1])

    def step(p, carry):
        y = pair(p)
        emit(2 * p - 2, carry[0] + y[2][0])
        emit(2 * p - 1, carry[1] + y[1][0] + y[2][1])
        return (y[0][0] + y[1][1], y[0][1])

    for p in range(1, rows // 2):
        carry = step(p, carry)


def row_mask(first, r, limit):
    g = first + r
    return jnp.where((g >= 0) & (g < limit), 1.0, 0.0).astype(F32)


def first_kernel(pos, w, own, prev, nxt, inner, slope):
    n = own.shape[0] - 6
    vol = (prev, own, nxt)

    def emit(r, pre):
        s = logistic(pre)
        act = pre * s
        inner[r] = (act * row_mask(pos[0] - 2, r, pos[1])).astype(BF16)
        slope[r] = (s + act * (1.0 - s)).astype(BF16)

    conv_rows(lambda a, i: vol[a][i], w, n + 6, emit, silu_in=True)


def grad_kernel(pos, w, slope, own, prev, nxt, grad):
    n = own.shape[0] - 4
    vol = (prev, own, nxt)

    def emit(r, value):
        out = value * slope[r + 1].astype(F32)
        grad[r] = (out * row_mask(pos[0] - 1, r, pos[1])).astype(BF16)

    conv_rows(lambda a, i: vol[a][i], w, n + 4, emit)


def video_kernel(pos, listed, w, wp, head, pool, base, own, prev, nxt, video, send, rim, sums):
    n = base.shape[0] - 6
    vol = (prev, own, nxt)

    def emit(r, value):
        out = (base[r + 2].astype(F32) + value) * row_mask(pos[0] - 1, r, pos[1])
        rim[r] = out.astype(BF16)

    conv_rows(lambda a, i: vol[a][i], w, n + 4, emit)

    def emit_plane(r, value):
        act = value * logistic(value) * head[...]
        sums[pl.ds(r, 1)] = jnp.sum(act, axis=0, keepdims=True)

    conv_rows(lambda a, i: rim[i], wp, n + 2, emit_plane, frames=1)

    def pool_row(i, _):
        a, b = rim[2 * i + 1], rim[2 * i + 2]
        video[2 * i] = a
        video[2 * i + 1] = b
        both = jnp.dot(jnp.concatenate([a, b], axis=1), pool[...], preferred_element_type=F32)
        half = both.shape[0] // 2
        lane = lax.broadcasted_iota(jnp.int32, (half, both.shape[1]), 1)
        packed = jnp.where(lane < both.shape[1] // 2, both[:half], both[half:])
        send[i, pl.ds(0, half)] = packed.astype(BF16)
        return 0

    lax.fori_loop(0, n // 2, pool_row, 0, unroll=8)

    dests = send.shape[0]
    groups = dests // LISTED
    quarter = n // groups
    base_row = send.shape[1] - quarter
    for k in range(LISTED):
        hit = jnp.where(listed[k] == pos[2], 1.0, 0.0).astype(F32)
        for q in range(groups):
            send[k * groups + q, pl.ds(base_row, quarter)] = (
                sums[q * quarter : (q + 1) * quarter] * hit
            ).astype(BF16)


def input_grad_kernel(w, cot, vin, own, prev, nxt, out):
    n = cot.shape[0]
    vol = (prev, own, nxt)

    def emit(r, value):
        x = vin[r].astype(F32)
        s = logistic(x)
        out[r] = (cot[r].astype(F32) + value * (s * (1.0 + x * (1.0 - s)))).astype(BF16)

    conv_rows(lambda a, i: vol[a][i], w, n + 2, emit)


def time_kernel_body(pos, listed, wt, mixer, head, recv, plane, score, total):
    frames = recv.shape[0]
    half, width = wt.shape[1] // 3, recv.shape[2]
    units = wt.shape[0] // 2
    plane[...] = recv[listed[pos[2] // (frames // LISTED)], pl.ds(half, plane.shape[0])].astype(F32)
    total[...] = jnp.zeros_like(total)
    lane = lax.broadcasted_iota(jnp.int32, (units, width), 1)

    def piece(t):
        if 0 <= t < frames:
            return recv[t, pl.ds(0, half)]
        return jnp.zeros((half, width), BF16)

    for i in range(frames // 2):
        f = [piece(2 * i + d) for d in (-1, 0, 1, 2)]
        rhs = jnp.concatenate(
            [jnp.concatenate(f[:3], axis=0), jnp.concatenate(f[1:], axis=0)], axis=1
        )
        y = jnp.dot(wt[...], rhs, preferred_element_type=F32)
        a, b = y[:, :width], y[:, width:]
        left = a[:units] + pltpu.roll(a[units:], width // 2, 1)
        right = pltpu.roll(b[:units], width // 2, 1) + b[units:]
        q = jnp.where(lane < width // 2, left, right)
        total[...] += q * logistic(q)

    both = total[...]
    mean = (both + pltpu.roll(both, width // 2, 1)) * (1.0 / frames)
    mixed = jnp.zeros_like(mean)
    rest = mean
    for _ in range(3):
        top = rest.astype(BF16)
        mixed = mixed + jnp.dot(mixer[...], top, preferred_element_type=F32)
        rest = rest - top.astype(F32)
    act = mixed * logistic(mixed) * head[...]
    score[...] = jnp.sum(act, axis=0, keepdims=True)[:, : width // 2]


def turned(x):
    return x.astype(F32).T.astype(BF16)


def weights_kernel(
    pos, ka, kb, kp, kt, km, hp, ht, wa, wb, wbt, wat, wp, wt, mixer, plane_row, time_row, pool
):
    odd = lax.rem(pos[2], 2)
    ch, width = plane_row.shape
    order = [jnp.where(odd == 1, a, 2 - a) for a in range(3)]
    for b in range(3):
        rows = pl.ds(b * ch, ch)
        for src, dst in ((ka, wa), (kb, wb)):
            dst[rows] = turned(jnp.concatenate([src[a, b, e] for a in order for e in range(3)], axis=0))
        for src, dst in ((kb, wbt), (ka, wat)):
            dst[rows] = jnp.concatenate([src[2 - a, 2 - b, 2 - e] for a in order for e in range(3)], axis=1)
        wp[rows] = turned(jnp.concatenate([kp[b, e] for e in range(3)], axis=0))
    half = ch // 2
    for i in range(2):
        part = [kt[a, pl.ds(i * half, half)] for a in range(3)]
        wt[pl.ds(i * ch, ch)] = turned(jnp.concatenate(part, axis=0))
    mixer[...] = turned(km[...])
    for src, dst in ((hp, plane_row), (ht, time_row)):
        dst[...] = jnp.broadcast_to(src[...].astype(F32), (width, ch)).T
    pairs = lax.broadcasted_iota(jnp.int32, pool.shape, 0) % width // 2
    lanes = lax.broadcasted_iota(jnp.int32, pool.shape, 1) % (width // 2)
    pool[...] = jnp.where(pairs == lanes, 0.25, 0.0).astype(BF16)


VMEM = pl.BlockSpec(memory_space=pltpu.VMEM)
SMEM = pl.BlockSpec(memory_space=pltpu.SMEM)


def call(body, outs, in_specs, scratch, flops, nbytes, limit=40):
    return pl.pallas_call(
        body,
        out_shape=outs,
        in_specs=in_specs,
        out_specs=jax.tree.map(lambda _: VMEM, outs),
        scratch_shapes=scratch,
        compiler_params=pltpu.CompilerParams(vmem_limit_bytes=limit * MIB),
        cost_estimate=pl.CostEstimate(flops=flops, bytes_accessed=nbytes, transcendentals=0),
    )


def swaps(size):
    pairs = [[(i, i + 1) for i in range(start, size - 1, 2)] for start in (0, 1)]
    return [p + [(j, i) for i, j in p] for p in pairs]


def shards(
    video_in,
    cotangent,
    kernel_a,
    kernel_b,
    plane_kernel,
    plane_head,
    time_kernel,
    time_mixer,
    time_head,
    listed,
):
    v, c = video_in[0], cotangent[0]
    n, ch, width = v.shape
    tm, sp = lax.axis_size("tm"), lax.axis_size("space")
    swap_first, swap_second = swaps(tm)
    me = lax.axis_index("tm")
    pos = jnp.stack([lax.axis_index("space") * n, sp * n, me]).astype(jnp.int32)

    def both(x):
        return lax.ppermute(x, "tm", swap_first), lax.ppermute(x, "tm", swap_second)

    even = lax.axis_index("space") % 2 == 0

    def edge(at_end):
        ends = [lax.dynamic_slice_in_dim(x, jnp.where(at_end, n - k, 0), k) for x, k in ((v, 3), (c, 2))]
        return jnp.concatenate(ends)

    row_first, row_second = swaps(sp)
    got = lax.ppermute(edge(even), "space", row_first)
    other = lax.ppermute(edge(~even), "space", row_second)
    up, dn = jnp.where(even, other, got), jnp.where(even, got, other)
    v_own = jnp.concatenate([up[:3], v, dn[:3]])
    c_own = jnp.concatenate([up[3:], c, dn[3:]])
    v_p, v_n = both(v_own)
    c_p, c_n = both(c_own)
    kernel_a, kernel_b, _ = lax.optimization_barrier((kernel_a, kernel_b, c_own))
    shapes = [((3 * ch, 9 * ch), BF16)] * 4 + [
        ((3 * ch, 3 * ch), BF16),
        ((2 * ch, 3 * ch // 2), BF16),
        ((ch, ch), BF16),
        ((ch, width), F32),
        ((ch, width), F32),
        ((2 * width, width), BF16),
    ]
    wa, wb, wbt, wat, wp, wt, mixer, plane_row, time_row, pool = call(
        weights_kernel,
        tuple(jax.ShapeDtypeStruct(shape, dtype) for shape, dtype in shapes),
        [SMEM] + [VMEM] * 7,
        [],
        10**7,
        2 * MIB,
    )(pos, kernel_a, kernel_b, plane_kernel, time_kernel, time_mixer, plane_head[None], time_head[None])

    def rows(r, dtype=BF16):
        return jax.ShapeDtypeStruct((r, ch, width), dtype)

    flops = 2 * 27 * ch * ch * width * n
    inner, slope = call(
        first_kernel, (rows(n + 4), rows(n + 4)), [SMEM] + [VMEM] * 4, [], flops, 6 * MIB
    )(pos, wa, v_own, v_p, v_n)
    in_p, in_n = both(inner)
    grad = call(
        grad_kernel, rows(n + 2), [SMEM] + [VMEM] * 5, [], flops, 6 * MIB
    )(pos, wbt, slope, c_own, c_p, c_n)
    gr_p, gr_n = both(grad)

    quarter = n // (tm // LISTED)
    video, send = call(
        video_kernel,
        (rows(n), jax.ShapeDtypeStruct((tm, ch // 2 + quarter, width), BF16)),
        [SMEM, SMEM] + [VMEM] * 8,
        [
            pltpu.VMEM((n + 2, ch, width), BF16),
            pltpu.VMEM((n, width), F32),
        ],
        flops * 4 // 3,
        6 * MIB,
    )(pos, listed, wb, wp, plane_row, pool, v_own, inner, in_p, in_n)
    recv = lax.all_to_all(send, "tm", split_axis=0, concat_axis=0, tiled=True)
    input_grad = call(input_grad_kernel, rows(n), [VMEM] * 6, [], flops, 6 * MIB)(
        wat, c, v, grad, gr_p, gr_n
    )
    plane_scores, time_scores = call(
        time_kernel_body,
        (jax.ShapeDtypeStruct((quarter, width), F32), jax.ShapeDtypeStruct((1, width // 2), F32)),
        [SMEM, SMEM, VMEM, VMEM, VMEM, VMEM],
        [pltpu.VMEM((ch, width), F32)],
        flops // 20,
        MIB,
    )(pos, listed, wt, mixer, time_row, recv)
    return (video[None], input_grad[None], plane_scores[None, None], time_scores[None])


def solution(mesh):
    return jax.shard_map(
        shards,
        mesh=mesh,
        in_specs=(P("tm", "space", None, None), P("tm", "space", None, None)) + (P(),) * 8,
        out_specs=(
            P("tm", "space", None, None),
            P("tm", "space", None, None),
            P("tm", "space", None, None),
            P("space", "tm", None),
        ),
        check_vma=False,
    )
```

```python
import functools

import jax
import jax.numpy as jnp
from jax import lax
from jax.experimental import pallas as pl
from jax.experimental.pallas import tpu as pltpu
from jax.sharding import PartitionSpec as P

LISTED = 8
F32 = jnp.float32
BF16 = jnp.bfloat16
MIB = 1 << 20


def logistic(x):
    return 0.5 + 0.5 * jnp.tanh(0.5 * x)


def shifted(x, lane):
    width = x.shape[1]
    left = jnp.where(lane == 0, jnp.zeros_like(x), pltpu.roll(x, 1, 1))
    right = jnp.where(lane == width - 1, jnp.zeros_like(x), pltpu.roll(x, width - 1, 1))
    return left, x, right


def taps(x, silu_in):
    x = x.astype(F32)
    lane = lax.broadcasted_iota(jnp.int32, x.shape, 1)
    if silu_in:
        x = x * logistic(x)
    return [t.astype(BF16) for t in shifted(x, lane)]


def conv_rows(load, weight, rows, emit, silu_in=False, frames=3):
    def pair(p):
        sides = []
        for j in range(2):
            parts = []
            for a in range(frames):
                parts += taps(load(a, 2 * p + j), silu_in)
            sides.append(jnp.concatenate(parts, axis=0))
        y = jnp.dot(weight, jnp.concatenate(sides, axis=1), preferred_element_type=F32)
        n, w = y.shape[0] // 3, y.shape[1] // 2
        return [[y[b * n : (b + 1) * n, j * w : (j + 1) * w] for j in range(2)] for b in range(3)]

    y = pair(0)
    carry = (y[0][0] + y[1][1], y[0][1])

    def step(p, carry):
        y = pair(p)
        emit(2 * p - 2, carry[0] + y[2][0])
        emit(2 * p - 1, carry[1] + y[1][0] + y[2][1])
        return (y[0][0] + y[1][1], y[0][1])

    for p in range(1, rows // 2):
        carry = step(p, carry)


def row_mask(first, r, limit):
    g = first + r
    return jnp.where((g >= 0) & (g < limit), 1.0, 0.0).astype(F32)


def first_kernel(pos, w, own, prev, nxt, inner, slope):
    n = own.shape[0] - 6
    vol = (prev, own, nxt)

    def emit(r, pre):
        s = logistic(pre)
        act = pre * s
        inner[r] = (act * row_mask(pos[0] - 2, r, pos[1])).astype(BF16)
        slope[r] = (s + act * (1.0 - s)).astype(BF16)

    conv_rows(lambda a, i: vol[a][i], w[...], n + 6, emit, silu_in=True)


def grad_kernel(pos, w, slope, own, prev, nxt, grad):
    n = own.shape[0] - 4
    vol = (prev, own, nxt)

    def emit(r, value):
        out = value * slope[r + 1].astype(F32)
        grad[r] = (out * row_mask(pos[0] - 1, r, pos[1])).astype(BF16)

    conv_rows(lambda a, i: vol[a][i], w[...], n + 4, emit)


def video_kernel(pos, listed, w, wp, head, pool, base, own, prev, nxt, video, send, rim, sums):
    n = base.shape[0] - 6
    vol = (prev, own, nxt)

    def emit(r, value):
        out = (base[r + 2].astype(F32) + value) * row_mask(pos[0] - 1, r, pos[1])
        rim[r] = out.astype(BF16)

    conv_rows(lambda a, i: vol[a][i], w[...], n + 4, emit)

    def emit_plane(r, value):
        act = value * logistic(value) * head[...]
        sums[pl.ds(r, 1)] = jnp.sum(act, axis=0, keepdims=True)

    conv_rows(lambda a, i: rim[i], wp[...], n + 2, emit_plane, frames=1)

    def pool_row(i, _):
        a, b = rim[2 * i + 1], rim[2 * i + 2]
        video[2 * i] = a
        video[2 * i + 1] = b
        both = jnp.dot(jnp.concatenate([a, b], axis=1), pool[...], preferred_element_type=F32)
        half = both.shape[0] // 2
        lane = lax.broadcasted_iota(jnp.int32, (half, both.shape[1]), 1)
        packed = jnp.where(lane < both.shape[1] // 2, both[:half], both[half:])
        send[i, pl.ds(0, half)] = packed.astype(BF16)
        return 0

    lax.fori_loop(0, n // 2, pool_row, 0, unroll=8)

    dests = send.shape[0]
    groups = dests // LISTED
    quarter = n // groups
    base_row = send.shape[1] - quarter
    for k in range(LISTED):
        hit = jnp.where(listed[k] == pos[2], 1.0, 0.0).astype(F32)
        for q in range(groups):
            send[k * groups + q, pl.ds(base_row, quarter)] = (
                sums[q * quarter : (q + 1) * quarter] * hit
            ).astype(BF16)


def near_kernel(w, near, own, part):
    vol = (near, own)

    def emit(r, value):
        part[r] = value

    conv_rows(lambda a, i: vol[a][i], w[:, : 2 * w.shape[1] // 3], own.shape[0], emit, frames=2)


def input_grad_kernel(w, cot, vin, part, far, out):
    def emit(r, value):
        x = vin[r].astype(F32)
        s = logistic(x)
        grad = (part[r] + value) * (s * (1.0 + x * (1.0 - s)))
        out[r] = (cot[r].astype(F32) + grad).astype(BF16)

    conv_rows(lambda a, i: far[i], w[:, 2 * w.shape[1] // 3 :], far.shape[0], emit, frames=1)


def time_kernel_body(pos, listed, wt, mixer, head, recv, plane, score, total):
    frames = recv.shape[0]
    half, width = wt.shape[1] // 3, recv.shape[2]
    units = wt.shape[0] // 2
    plane[...] = recv[listed[pos[2] // (frames // LISTED)], pl.ds(half, plane.shape[0])].astype(F32)
    total[...] = jnp.zeros_like(total)
    lane = lax.broadcasted_iota(jnp.int32, (units, width), 1)

    def piece(t):
        if 0 <= t < frames:
            return recv[t, pl.ds(0, half)]
        return jnp.zeros((half, width), BF16)

    for i in range(frames // 2):
        f = [piece(2 * i + d) for d in (-1, 0, 1, 2)]
        rhs = jnp.concatenate(
            [jnp.concatenate(f[:3], axis=0), jnp.concatenate(f[1:], axis=0)], axis=1
        )
        y = jnp.dot(wt[...], rhs, preferred_element_type=F32)
        a, b = y[:, :width], y[:, width:]
        left = a[:units] + pltpu.roll(a[units:], width // 2, 1)
        right = pltpu.roll(b[:units], width // 2, 1) + b[units:]
        q = jnp.where(lane < width // 2, left, right)
        total[...] += q * logistic(q)

    both = total[...]
    mean = (both + pltpu.roll(both, width // 2, 1)) * (1.0 / frames)
    mixed = jnp.zeros_like(mean)
    rest = mean
    for _ in range(3):
        top = rest.astype(BF16)
        mixed = mixed + jnp.dot(mixer[...], top, preferred_element_type=F32)
        rest = rest - top.astype(F32)
    act = mixed * logistic(mixed) * head[...]
    score[...] = jnp.sum(act, axis=0, keepdims=True)[:, : width // 2]


def turned(x):
    return x.astype(F32).T.astype(BF16)


def weights_kernel(
    pos, ka, kb, kp, kt, km, hp, ht, wa, wb, wbt, wat, wp, wt, mixer, plane_row, time_row, pool
):
    odd = lax.rem(pos[2], 2)
    ch, width = plane_row.shape
    order = [jnp.where(odd == 1, a, 2 - a) for a in range(3)]
    for b in range(3):
        rows = pl.ds(b * ch, ch)
        for src, dst in ((ka, wa), (kb, wb)):
            dst[rows] = turned(jnp.concatenate([src[a, b, e] for a in order for e in range(3)], axis=0))
        for src, dst in ((kb, wbt), (ka, wat)):
            dst[rows] = jnp.concatenate([src[2 - a, 2 - b, 2 - e] for a in order for e in range(3)], axis=1)
        wp[rows] = turned(jnp.concatenate([kp[b, e] for e in range(3)], axis=0))
    half = ch // 2
    for i in range(2):
        part = [kt[a, pl.ds(i * half, half)] for a in range(3)]
        wt[pl.ds(i * ch, ch)] = turned(jnp.concatenate(part, axis=0))
    mixer[...] = turned(km[...])
    for src, dst in ((hp, plane_row), (ht, time_row)):
        dst[...] = jnp.broadcast_to(src[...].astype(F32), (width, ch)).T
    pairs = lax.broadcasted_iota(jnp.int32, pool.shape, 0) % width // 2
    lanes = lax.broadcasted_iota(jnp.int32, pool.shape, 1) % (width // 2)
    pool[...] = jnp.where(pairs == lanes, 0.25, 0.0).astype(BF16)


VMEM = pl.BlockSpec(memory_space=pltpu.VMEM)
SMEM = pl.BlockSpec(memory_space=pltpu.SMEM)


def call(body, outs, in_specs, scratch, flops, nbytes, limit=40):
    return pl.pallas_call(
        body,
        out_shape=outs,
        in_specs=in_specs,
        out_specs=jax.tree.map(lambda _: VMEM, outs),
        scratch_shapes=scratch,
        compiler_params=pltpu.CompilerParams(vmem_limit_bytes=limit * MIB),
        cost_estimate=pl.CostEstimate(flops=flops, bytes_accessed=nbytes, transcendentals=0),
    )


def swaps(size):
    pairs = [[(i, i + 1) for i in range(start, size - 1, 2)] for start in (0, 1)]
    return [p + [(j, i) for i, j in p] for p in pairs]


def shards(
    video_in,
    cotangent,
    kernel_a,
    kernel_b,
    plane_kernel,
    plane_head,
    time_kernel,
    time_mixer,
    time_head,
    listed,
):
    v, c = video_in[0], cotangent[0]
    n, ch, width = v.shape
    tm, sp = lax.axis_size("tm"), lax.axis_size("space")
    swap_first, swap_second = swaps(tm)
    me = lax.axis_index("tm")
    pos = jnp.stack([lax.axis_index("space") * n, sp * n, me]).astype(jnp.int32)

    def both(x):
        far = lax.ppermute(x, "tm", swap_second)
        return lax.ppermute(x, "tm", swap_first), far

    even = lax.axis_index("space") % 2 == 0

    def edge(at_end):
        ends = [lax.dynamic_slice_in_dim(x, jnp.where(at_end, n - k, 0), k) for x, k in ((v, 3), (c, 2))]
        return jnp.concatenate(ends)

    row_first, row_second = swaps(sp)
    got = lax.ppermute(edge(even), "space", row_first)
    other = lax.ppermute(edge(~even), "space", row_second)
    up, dn = jnp.where(even, other, got), jnp.where(even, got, other)
    v_own = jnp.concatenate([up[:3], v, dn[:3]])
    c_own = jnp.concatenate([up[3:], c, dn[3:]])
    v_p, v_n = both(v_own)
    c_p, c_n = both(c_own)
    kernel_a, kernel_b, _ = lax.optimization_barrier((kernel_a, kernel_b, c_own))
    shapes = [((3 * ch, 9 * ch), BF16)] * 4 + [
        ((3 * ch, 3 * ch), BF16),
        ((2 * ch, 3 * ch // 2), BF16),
        ((ch, ch), BF16),
        ((ch, width), F32),
        ((ch, width), F32),
        ((2 * width, width), BF16),
    ]
    wa, wb, wbt, wat, wp, wt, mixer, plane_row, time_row, pool = call(
        weights_kernel,
        tuple(jax.ShapeDtypeStruct(shape, dtype) for shape, dtype in shapes),
        [SMEM] + [VMEM] * 7,
        [],
        10**7,
        2 * MIB,
    )(pos, kernel_a, kernel_b, plane_kernel, time_kernel, time_mixer, plane_head[None], time_head[None])

    def rows(r, dtype=BF16):
        return jax.ShapeDtypeStruct((r, ch, width), dtype)

    flops = 2 * 27 * ch * ch * width * n
    inner, slope = call(
        first_kernel, (rows(n + 4), rows(n + 4)), [SMEM] + [VMEM] * 4, [], flops, 6 * MIB
    )(pos, wa, v_own, v_p, v_n)
    in_p, in_n = both(inner)
    grad = call(
        grad_kernel, rows(n + 2), [SMEM] + [VMEM] * 5, [], flops, 6 * MIB
    )(pos, wbt, slope, c_own, c_p, c_n)
    gr_p, gr_n = both(grad)

    quarter = n // (tm // LISTED)
    video, send = call(
        video_kernel,
        (rows(n), jax.ShapeDtypeStruct((tm, ch // 2 + quarter, width), BF16)),
        [SMEM, SMEM] + [VMEM] * 8,
        [
            pltpu.VMEM((n + 2, ch, width), BF16),
            pltpu.VMEM((n, width), F32),
        ],
        flops * 4 // 3,
        6 * MIB,
    )(pos, listed, wb, wp, plane_row, pool, v_own, inner, in_p, in_n)
    recv = lax.all_to_all(send, "tm", split_axis=0, concat_axis=0, tiled=True)
    part = call(
        near_kernel, jax.ShapeDtypeStruct((n, ch, width), F32), [VMEM] * 3, [], flops * 2 // 3, 6 * MIB
    )(wat, gr_p, grad)
    input_grad = call(input_grad_kernel, rows(n), [VMEM] * 5, [], flops // 3, 6 * MIB)(
        wat, c, v, part, gr_n
    )
    plane_scores, time_scores = call(
        time_kernel_body,
        (jax.ShapeDtypeStruct((quarter, width), F32), jax.ShapeDtypeStruct((1, width // 2), F32)),
        [SMEM, SMEM, VMEM, VMEM, VMEM, VMEM],
        [pltpu.VMEM((ch, width), F32)],
        flops // 20,
        MIB,
    )(pos, listed, wt, mixer, time_row, recv)
    return (video[None], input_grad[None], plane_scores[None, None], time_scores[None])


def solution(mesh):
    return jax.shard_map(
        shards,
        mesh=mesh,
        in_specs=(P("tm", "space", None, None), P("tm", "space", None, None)) + (P(),) * 8,
        out_specs=(
            P("tm", "space", None, None),
            P("tm", "space", None, None),
            P("tm", "space", None, None),
            P("space", "tm", None),
        ),
        check_vma=False,
    )
```

```python
import functools

import jax
import jax.numpy as jnp
from jax import lax
from jax.experimental import pallas as pl
from jax.experimental.pallas import tpu as pltpu
from jax.sharding import PartitionSpec as P

LISTED = 8
F32 = jnp.float32
BF16 = jnp.bfloat16
MIB = 1 << 20


def logistic(x):
    return 0.5 + 0.5 * jnp.tanh(0.5 * x)


def shifted(x, lane):
    width = x.shape[1]
    left = jnp.where(lane == 0, jnp.zeros_like(x), pltpu.roll(x, 1, 1))
    right = jnp.where(lane == width - 1, jnp.zeros_like(x), pltpu.roll(x, width - 1, 1))
    return left, x, right


def taps(x, silu_in):
    lane = lax.broadcasted_iota(jnp.int32, x.shape, 1)
    if silu_in:
        x = x.astype(F32)
        x = (x * logistic(x)).astype(BF16)
    return list(shifted(x, lane))


def conv_rows(load, weight, rows, emit, silu_in=False, frames=3):
    def pair(p):
        sides = []
        for j in range(2):
            parts = []
            for a in range(frames):
                parts += taps(load(a, 2 * p + j), silu_in)
            sides.append(jnp.concatenate(parts, axis=0))
        y = jnp.dot(weight, jnp.concatenate(sides, axis=1), preferred_element_type=F32)
        n, w = y.shape[0] // 3, y.shape[1] // 2
        return [[y[b * n : (b + 1) * n, j * w : (j + 1) * w] for j in range(2)] for b in range(3)]

    y = pair(0)
    carry = (y[0][0] + y[1][1], y[0][1])

    def step(p, carry):
        y = pair(p)
        emit(2 * p - 2, carry[0] + y[2][0])
        emit(2 * p - 1, carry[1] + y[1][0] + y[2][1])
        return (y[0][0] + y[1][1], y[0][1])

    for p in range(1, rows // 2):
        carry = step(p, carry)


def row_mask(first, r, limit):
    g = first + r
    return jnp.where((g >= 0) & (g < limit), 1.0, 0.0).astype(F32)


def first_kernel(pos, w, own, prev, nxt, inner, slope):
    n = own.shape[0] - 6
    vol = (prev, own, nxt)

    def emit(r, pre):
        s = logistic(pre)
        act = pre * s
        inner[r] = (act * row_mask(pos[0] - 2, r, pos[1])).astype(BF16)
        slope[r] = (s + act * (1.0 - s)).astype(BF16)

    conv_rows(lambda a, i: vol[a][i], w[...], n + 6, emit, silu_in=True)


def grad_kernel(pos, w, slope, own, prev, nxt, grad):
    n = own.shape[0] - 4
    vol = (prev, own, nxt)

    def emit(r, value):
        out = value * slope[r + 1].astype(F32)
        grad[r] = (out * row_mask(pos[0] - 1, r, pos[1])).astype(BF16)

    conv_rows(lambda a, i: vol[a][i], w[...], n + 4, emit)


def video_kernel(pos, listed, w, wp, head, pool, base, own, prev, nxt, video, send, rim, sums):
    n = base.shape[0] - 6
    vol = (prev, own, nxt)

    def emit(r, value):
        out = (base[r + 2].astype(F32) + value) * row_mask(pos[0] - 1, r, pos[1])
        rim[r] = out.astype(BF16)

    conv_rows(lambda a, i: vol[a][i], w[...], n + 4, emit)

    def emit_plane(r, value):
        act = value * logistic(value) * head[...]
        sums[pl.ds(r, 1)] = jnp.sum(act, axis=0, keepdims=True)

    conv_rows(lambda a, i: rim[i], wp[...], n + 2, emit_plane, frames=1)

    def pool_row(i, _):
        a, b = rim[2 * i + 1], rim[2 * i + 2]
        video[2 * i] = a
        video[2 * i + 1] = b
        both = jnp.dot(jnp.concatenate([a, b], axis=1), pool[...], preferred_element_type=F32)
        half = both.shape[0] // 2
        lane = lax.broadcasted_iota(jnp.int32, (half, both.shape[1]), 1)
        packed = jnp.where(lane < both.shape[1] // 2, both[:half], both[half:])
        send[i, pl.ds(0, half)] = packed.astype(BF16)
        return 0

    lax.fori_loop(0, n // 2, pool_row, 0, unroll=8)

    dests = send.shape[0]
    groups = dests // LISTED
    quarter = n // groups
    base_row = send.shape[1] - quarter
    for k in range(LISTED):
        hit = jnp.where(listed[k] == pos[2], 1.0, 0.0).astype(F32)
        for q in range(groups):
            send[k * groups + q, pl.ds(base_row, quarter)] = (
                sums[q * quarter : (q + 1) * quarter] * hit
            ).astype(BF16)


def near_kernel(w, near, own, part):
    vol = (near, own)

    def emit(r, value):
        part[r] = value

    conv_rows(lambda a, i: vol[a][i], w[:, : 2 * w.shape[1] // 3], own.shape[0], emit, frames=2)


def input_grad_kernel(w, cot, vin, part, far, out):
    def emit(r, value):
        x = vin[r].astype(F32)
        s = logistic(x)
        grad = (part[r] + value) * (s * (1.0 + x * (1.0 - s)))
        out[r] = (cot[r].astype(F32) + grad).astype(BF16)

    conv_rows(lambda a, i: far[i], w[:, 2 * w.shape[1] // 3 :], far.shape[0], emit, frames=1)


def time_kernel_body(pos, listed, wt, mixer, head, recv, plane, score):
    frames = recv.shape[0]
    half, width = wt.shape[1] // 3, recv.shape[2]
    units = wt.shape[0] // 2
    plane[...] = recv[listed[pos[2] // (frames // LISTED)], pl.ds(half, plane.shape[0])].astype(F32)
    total = jnp.zeros((units, width), F32)
    lane = lax.broadcasted_iota(jnp.int32, (units, width), 1)

    def piece(t):
        if 0 <= t < frames:
            return recv[t, pl.ds(0, half)]
        return jnp.zeros((half, width), BF16)

    for i in range(frames // 2):
        f = [piece(2 * i + d) for d in (-1, 0, 1, 2)]
        rhs = jnp.concatenate(
            [jnp.concatenate(f[:3], axis=0), jnp.concatenate(f[1:], axis=0)], axis=1
        )
        y = jnp.dot(wt[...], rhs, preferred_element_type=F32)
        a, b = y[:, :width], y[:, width:]
        left = a[:units] + pltpu.roll(a[units:], width // 2, 1)
        right = pltpu.roll(b[:units], width // 2, 1) + b[units:]
        q = jnp.where(lane < width // 2, left, right)
        total = total + q * logistic(q)

    mean = (total + pltpu.roll(total, width // 2, 1)) * (1.0 / frames)
    parts, rest = [], mean
    for _ in range(3):
        parts.append(rest.astype(BF16))
        rest = rest - parts[-1].astype(F32)
    mixers = jnp.concatenate([mixer[...]] * 3, axis=1)
    mixed = jnp.dot(mixers, jnp.concatenate(parts, axis=0), preferred_element_type=F32)
    act = mixed * logistic(mixed) * head[...]
    score[...] = jnp.sum(act, axis=0, keepdims=True)[:, : width // 2]


def turned(x):
    return x.astype(F32).T.astype(BF16)


def weights_kernel(
    pos, ka, kb, kp, kt, km, hp, ht, wa, wb, wbt, wat, wp, wt, mixer, plane_row, time_row, pool
):
    odd = lax.rem(pos[2], 2)
    ch, width = plane_row.shape
    order = [jnp.where(odd == 1, a, 2 - a) for a in range(3)]
    for b in range(3):
        rows = pl.ds(b * ch, ch)
        for src, dst in ((ka, wa), (kb, wb)):
            dst[rows] = turned(jnp.concatenate([src[a, b, e] for a in order for e in range(3)], axis=0))
        for src, dst in ((kb, wbt), (ka, wat)):
            dst[rows] = jnp.concatenate([src[2 - a, 2 - b, 2 - e] for a in order for e in range(3)], axis=1)
        wp[rows] = turned(jnp.concatenate([kp[b, e] for e in range(3)], axis=0))
    half = ch // 2
    for i in range(2):
        part = [kt[a, pl.ds(i * half, half)] for a in range(3)]
        wt[pl.ds(i * ch, ch)] = turned(jnp.concatenate(part, axis=0))
    mixer[...] = turned(km[...])
    for src, dst in ((hp, plane_row), (ht, time_row)):
        dst[...] = jnp.broadcast_to(src[...].astype(F32), (width, ch)).T
    pairs = lax.broadcasted_iota(jnp.int32, pool.shape, 0) % width // 2
    lanes = lax.broadcasted_iota(jnp.int32, pool.shape, 1) % (width // 2)
    pool[...] = jnp.where(pairs == lanes, 0.25, 0.0).astype(BF16)


VMEM = pl.BlockSpec(memory_space=pltpu.VMEM)
SMEM = pl.BlockSpec(memory_space=pltpu.SMEM)


def call(body, outs, in_specs, scratch, flops, nbytes, limit=40):
    return pl.pallas_call(
        body,
        out_shape=outs,
        in_specs=in_specs,
        out_specs=jax.tree.map(lambda _: VMEM, outs),
        scratch_shapes=scratch,
        compiler_params=pltpu.CompilerParams(vmem_limit_bytes=limit * MIB),
        cost_estimate=pl.CostEstimate(flops=flops, bytes_accessed=nbytes, transcendentals=0),
    )


def swaps(size):
    pairs = [[(i, i + 1) for i in range(start, size - 1, 2)] for start in (0, 1)]
    return [p + [(j, i) for i, j in p] for p in pairs]


def shards(
    video_in,
    cotangent,
    kernel_a,
    kernel_b,
    plane_kernel,
    plane_head,
    time_kernel,
    time_mixer,
    time_head,
    listed,
):
    v, c = video_in[0], cotangent[0]
    n, ch, width = v.shape
    tm, sp = lax.axis_size("tm"), lax.axis_size("space")
    swap_first, swap_second = swaps(tm)
    me = lax.axis_index("tm")
    pos = jnp.stack([lax.axis_index("space") * n, sp * n, me]).astype(jnp.int32)

    def both(x):
        far = lax.ppermute(x, "tm", swap_second)
        return lax.ppermute(x, "tm", swap_first), far

    even = lax.axis_index("space") % 2 == 0

    def edge(at_end):
        ends = [lax.dynamic_slice_in_dim(x, jnp.where(at_end, n - k, 0), k) for x, k in ((v, 3), (c, 2))]
        return jnp.concatenate(ends)

    row_first, row_second = swaps(sp)
    got = lax.ppermute(edge(even), "space", row_first)
    other = lax.ppermute(edge(~even), "space", row_second)
    up, dn = jnp.where(even, other, got), jnp.where(even, got, other)
    v_own = jnp.concatenate([up[:3], v, dn[:3]])
    c_own = jnp.concatenate([up[3:], c, dn[3:]])
    v_p, v_n = both(v_own)
    c_p, c_n = both(c_own)
    kernel_a, kernel_b, _ = lax.optimization_barrier((kernel_a, kernel_b, c_own))
    shapes = [((3 * ch, 9 * ch), BF16)] * 4 + [
        ((3 * ch, 3 * ch), BF16),
        ((2 * ch, 3 * ch // 2), BF16),
        ((ch, ch), BF16),
        ((ch, width), F32),
        ((ch, width), F32),
        ((2 * width, width), BF16),
    ]
    wa, wb, wbt, wat, wp, wt, mixer, plane_row, time_row, pool = call(
        weights_kernel,
        tuple(jax.ShapeDtypeStruct(shape, dtype) for shape, dtype in shapes),
        [SMEM] + [VMEM] * 7,
        [],
        10**7,
        2 * MIB,
    )(pos, kernel_a, kernel_b, plane_kernel, time_kernel, time_mixer, plane_head[None], time_head[None])

    def rows(r, dtype=BF16):
        return jax.ShapeDtypeStruct((r, ch, width), dtype)

    flops = 2 * 27 * ch * ch * width * n
    inner, slope = call(
        first_kernel, (rows(n + 4), rows(n + 4)), [SMEM] + [VMEM] * 4, [], flops, 6 * MIB
    )(pos, wa, v_own, v_p, v_n)
    in_p, in_n = both(inner)
    grad = call(
        grad_kernel, rows(n + 2), [SMEM] + [VMEM] * 5, [], flops, 6 * MIB
    )(pos, wbt, slope, c_own, c_p, c_n)
    gr_p, gr_n = both(grad)

    quarter = n // (tm // LISTED)
    video, send = call(
        video_kernel,
        (rows(n), jax.ShapeDtypeStruct((tm, ch // 2 + quarter, width), BF16)),
        [SMEM, SMEM] + [VMEM] * 8,
        [
            pltpu.VMEM((n + 2, ch, width), BF16),
            pltpu.VMEM((n, width), F32),
        ],
        flops * 4 // 3,
        6 * MIB,
    )(pos, listed, wb, wp, plane_row, pool, v_own, inner, in_p, in_n)
    recv = lax.all_to_all(send, "tm", split_axis=0, concat_axis=0, tiled=True)
    part = call(
        near_kernel, jax.ShapeDtypeStruct((n, ch, width), F32), [VMEM] * 3, [], flops * 2 // 3, 6 * MIB
    )(wat, gr_p, grad)
    input_grad = call(input_grad_kernel, rows(n), [VMEM] * 5, [], flops // 3, 6 * MIB)(
        wat, c, v, part, gr_n
    )
    plane_scores, time_scores = call(
        time_kernel_body,
        (jax.ShapeDtypeStruct((quarter, width), F32), jax.ShapeDtypeStruct((1, width // 2), F32)),
        [SMEM, SMEM, VMEM, VMEM, VMEM, VMEM],
        [],
        flops // 20,
        MIB,
    )(pos, listed, wt, mixer, time_row, recv)
    return (video[None], input_grad[None], plane_scores[None, None], time_scores[None])


def solution(mesh):
    return jax.shard_map(
        shards,
        mesh=mesh,
        in_specs=(P("tm", "space", None, None), P("tm", "space", None, None)) + (P(),) * 8,
        out_specs=(
            P("tm", "space", None, None),
            P("tm", "space", None, None),
            P("tm", "space", None, None),
            P("space", "tm", None),
        ),
        check_vma=False,
    )
```

```python
import functools

import jax
import jax.numpy as jnp
from jax import lax
from jax.experimental import pallas as pl
from jax.experimental.pallas import tpu as pltpu
from jax.sharding import PartitionSpec as P

LISTED = 8
F32 = jnp.float32
BF16 = jnp.bfloat16
MIB = 1 << 20


def logistic(x):
    return 0.5 + 0.5 * jnp.tanh(0.5 * x)


def shifted(x, lane):
    width = x.shape[1]
    left = jnp.where(lane == 0, jnp.zeros_like(x), pltpu.roll(x, 1, 1))
    right = jnp.where(lane == width - 1, jnp.zeros_like(x), pltpu.roll(x, width - 1, 1))
    return left, x, right


def taps(x, silu_in):
    lane = lax.broadcasted_iota(jnp.int32, x.shape, 1)
    if silu_in:
        x = x.astype(F32)
        x = (x * logistic(x)).astype(BF16)
    return list(shifted(x, lane))


def conv_rows(load, weight, rows, emit, silu_in=False, frames=3):
    def pair(p):
        sides = []
        for j in range(2):
            parts = []
            for a in range(frames):
                parts += taps(load(a, 2 * p + j), silu_in)
            sides.append(jnp.concatenate(parts, axis=0))
        y = jnp.dot(weight, jnp.concatenate(sides, axis=1), preferred_element_type=F32)
        n, w = y.shape[0] // 3, y.shape[1] // 2
        return [[y[b * n : (b + 1) * n, j * w : (j + 1) * w] for j in range(2)] for b in range(3)]

    y = pair(0)
    carry = (y[0][0] + y[1][1], y[0][1])

    def step(p, carry):
        y = pair(p)
        emit(2 * p - 2, carry[0] + y[2][0])
        emit(2 * p - 1, carry[1] + y[1][0] + y[2][1])
        return (y[0][0] + y[1][1], y[0][1])

    for p in range(1, rows // 2):
        carry = step(p, carry)


def row_mask(first, r, limit):
    g = first + r
    return jnp.where((g >= 0) & (g < limit), 1.0, 0.0).astype(F32)


def first_kernel(pos, w, own, prev, nxt, inner, slope):
    n = own.shape[0] - 6
    vol = (prev, own, nxt)

    def emit(r, pre):
        s = logistic(pre)
        act = pre * s
        inner[r] = (act * row_mask(pos[0] - 2, r, pos[1])).astype(BF16)
        slope[r] = (s + act * (1.0 - s)).astype(BF16)

    conv_rows(lambda a, i: vol[a][i], w[...], n + 6, emit, silu_in=True)


def grad_kernel(pos, w, slope, own, prev, nxt, grad):
    n = own.shape[0] - 4
    vol = (prev, own, nxt)

    def emit(r, value):
        out = value * slope[r + 1].astype(F32)
        grad[r] = (out * row_mask(pos[0] - 1, r, pos[1])).astype(BF16)

    conv_rows(lambda a, i: vol[a][i], w[...], n + 4, emit)


def video_kernel(pos, listed, w, wp, head, pool, base, own, prev, nxt, video, send, rim, sums):
    n = base.shape[0] - 6
    vol = (prev, own, nxt)

    def emit(r, value):
        out = (base[r + 2].astype(F32) + value) * row_mask(pos[0] - 1, r, pos[1])
        rim[r] = out.astype(BF16)

    conv_rows(lambda a, i: vol[a][i], w[...], n + 4, emit)

    def emit_plane(r, value):
        act = value * logistic(value) * head[...]
        sums[pl.ds(r, 1)] = jnp.sum(act, axis=0, keepdims=True)

    conv_rows(lambda a, i: rim[i], wp[...], n + 2, emit_plane, frames=1)

    def pool_row(i, _):
        a, b = rim[2 * i + 1], rim[2 * i + 2]
        video[2 * i] = a
        video[2 * i + 1] = b
        both = jnp.dot(jnp.concatenate([a, b], axis=1), pool[...], preferred_element_type=F32)
        half = both.shape[0] // 2
        lane = lax.broadcasted_iota(jnp.int32, (half, both.shape[1]), 1)
        packed = jnp.where(lane < both.shape[1] // 2, both[:half], both[half:])
        send[i, pl.ds(0, half)] = packed.astype(BF16)
        return 0

    lax.fori_loop(0, n // 2, pool_row, 0, unroll=8)

    dests = send.shape[0]
    groups = dests // LISTED
    quarter = n // groups
    base_row = send.shape[1] - quarter
    for k in range(LISTED):
        hit = jnp.where(listed[k] == pos[2], 1.0, 0.0).astype(F32)
        for q in range(groups):
            send[k * groups + q, pl.ds(base_row, quarter)] = (
                sums[q * quarter : (q + 1) * quarter] * hit
            ).astype(BF16)


def near_kernel(w, near, own, cot, vin, part, slope):
    vol = (near, own)

    def emit(r, value):
        x = vin[r].astype(F32)
        s = logistic(x)
        rise = s * (1.0 + x * (1.0 - s))
        slope[r] = rise
        part[r] = cot[r].astype(F32) + value * rise

    conv_rows(lambda a, i: vol[a][i], w[:, : 2 * w.shape[1] // 3], own.shape[0], emit, frames=2)


def input_grad_kernel(w, part, slope, far, out):
    def emit(r, value):
        out[r] = (part[r] + value * slope[r]).astype(BF16)

    conv_rows(lambda a, i: far[i], w[:, 2 * w.shape[1] // 3 :], far.shape[0], emit, frames=1)


def time_kernel_body(pos, listed, wt, mixer, head, recv, plane, score):
    frames = recv.shape[0]
    half, width = wt.shape[1] // 3, recv.shape[2]
    units = wt.shape[0] // 2
    plane[...] = recv[listed[pos[2] // (frames // LISTED)], pl.ds(half, plane.shape[0])].astype(F32)
    total = jnp.zeros((units, width), F32)
    lane = lax.broadcasted_iota(jnp.int32, (units, width), 1)

    def piece(t):
        if 0 <= t < frames:
            return recv[t, pl.ds(0, half)]
        return jnp.zeros((half, width), BF16)

    for i in range(frames // 2):
        f = [piece(2 * i + d) for d in (-1, 0, 1, 2)]
        rhs = jnp.concatenate(
            [jnp.concatenate(f[:3], axis=0), jnp.concatenate(f[1:], axis=0)], axis=1
        )
        y = jnp.dot(wt[...], rhs, preferred_element_type=F32)
        a, b = y[:, :width], y[:, width:]
        left = a[:units] + pltpu.roll(a[units:], width // 2, 1)
        right = pltpu.roll(b[:units], width // 2, 1) + b[units:]
        q = jnp.where(lane < width // 2, left, right)
        total = total + q * logistic(q)

    mean = (total + pltpu.roll(total, width // 2, 1)) * (1.0 / frames)
    parts, rest = [], mean
    for _ in range(3):
        parts.append(rest.astype(BF16))
        rest = rest - parts[-1].astype(F32)
    mixers = jnp.concatenate([mixer[...]] * 3, axis=1)
    mixed = jnp.dot(mixers, jnp.concatenate(parts, axis=0), preferred_element_type=F32)
    act = mixed * logistic(mixed) * head[...]
    score[...] = jnp.sum(act, axis=0, keepdims=True)[:, : width // 2]


def turned(x):
    return x.astype(F32).T.astype(BF16)


def weights_kernel(
    pos, ka, kb, kp, kt, km, hp, ht, wa, wb, wbt, wat, wp, wt, mixer, plane_row, time_row, pool
):
    odd = lax.rem(pos[2], 2)
    ch, width = plane_row.shape
    order = [jnp.where(odd == 1, a, 2 - a) for a in range(3)]
    for b in range(3):
        rows = pl.ds(b * ch, ch)
        for src, dst in ((ka, wa), (kb, wb)):
            dst[rows] = turned(jnp.concatenate([src[a, b, e] for a in order for e in range(3)], axis=0))
        for src, dst in ((kb, wbt), (ka, wat)):
            dst[rows] = jnp.concatenate([src[2 - a, 2 - b, 2 - e] for a in order for e in range(3)], axis=1)
        wp[rows] = turned(jnp.concatenate([kp[b, e] for e in range(3)], axis=0))
    half = ch // 2
    for i in range(2):
        part = [kt[a, pl.ds(i * half, half)] for a in range(3)]
        wt[pl.ds(i * ch, ch)] = turned(jnp.concatenate(part, axis=0))
    mixer[...] = turned(km[...])
    for src, dst in ((hp, plane_row), (ht, time_row)):
        dst[...] = jnp.broadcast_to(src[...].astype(F32), (width, ch)).T
    pairs = lax.broadcasted_iota(jnp.int32, pool.shape, 0) % width // 2
    lanes = lax.broadcasted_iota(jnp.int32, pool.shape, 1) % (width // 2)
    pool[...] = jnp.where(pairs == lanes, 0.25, 0.0).astype(BF16)


VMEM = pl.BlockSpec(memory_space=pltpu.VMEM)
SMEM = pl.BlockSpec(memory_space=pltpu.SMEM)


def call(body, outs, in_specs, scratch, flops, nbytes, limit=40):
    return pl.pallas_call(
        body,
        out_shape=outs,
        in_specs=in_specs,
        out_specs=jax.tree.map(lambda _: VMEM, outs),
        scratch_shapes=scratch,
        compiler_params=pltpu.CompilerParams(vmem_limit_bytes=limit * MIB),
        cost_estimate=pl.CostEstimate(flops=flops, bytes_accessed=nbytes, transcendentals=0),
    )


def swaps(size):
    pairs = [[(i, i + 1) for i in range(start, size - 1, 2)] for start in (0, 1)]
    return [p + [(j, i) for i, j in p] for p in pairs]


def shards(
    video_in,
    cotangent,
    kernel_a,
    kernel_b,
    plane_kernel,
    plane_head,
    time_kernel,
    time_mixer,
    time_head,
    listed,
):
    v, c = video_in[0], cotangent[0]
    n, ch, width = v.shape
    tm, sp = lax.axis_size("tm"), lax.axis_size("space")
    swap_first, swap_second = swaps(tm)
    me = lax.axis_index("tm")
    pos = jnp.stack([lax.axis_index("space") * n, sp * n, me]).astype(jnp.int32)

    def both(x):
        far = lax.ppermute(x, "tm", swap_second)
        return lax.ppermute(x, "tm", swap_first), far

    even = lax.axis_index("space") % 2 == 0

    def edge(at_end):
        ends = [lax.dynamic_slice_in_dim(x, jnp.where(at_end, n - k, 0), k) for x, k in ((v, 3), (c, 2))]
        return jnp.concatenate(ends)

    row_first, row_second = swaps(sp)
    got = lax.ppermute(edge(even), "space", row_first)
    other = lax.ppermute(edge(~even), "space", row_second)
    up, dn = jnp.where(even, other, got), jnp.where(even, got, other)
    v_own = jnp.concatenate([up[:3], v, dn[:3]])
    c_own = jnp.concatenate([up[3:], c, dn[3:]])
    v_p, v_n = both(v_own)
    c_p, c_n = both(c_own)
    kernel_a, kernel_b, _ = lax.optimization_barrier((kernel_a, kernel_b, c_own))
    shapes = [((3 * ch, 9 * ch), BF16)] * 4 + [
        ((3 * ch, 3 * ch), BF16),
        ((2 * ch, 3 * ch // 2), BF16),
        ((ch, ch), BF16),
        ((ch, width), F32),
        ((ch, width), F32),
        ((2 * width, width), BF16),
    ]
    wa, wb, wbt, wat, wp, wt, mixer, plane_row, time_row, pool = call(
        weights_kernel,
        tuple(jax.ShapeDtypeStruct(shape, dtype) for shape, dtype in shapes),
        [SMEM] + [VMEM] * 7,
        [],
        10**7,
        2 * MIB,
    )(pos, kernel_a, kernel_b, plane_kernel, time_kernel, time_mixer, plane_head[None], time_head[None])

    def rows(r, dtype=BF16):
        return jax.ShapeDtypeStruct((r, ch, width), dtype)

    flops = 2 * 27 * ch * ch * width * n
    inner, slope = call(
        first_kernel, (rows(n + 4), rows(n + 4)), [SMEM] + [VMEM] * 4, [], flops, 6 * MIB
    )(pos, wa, v_own, v_p, v_n)
    in_p, in_n = both(inner)
    grad = call(
        grad_kernel, rows(n + 2), [SMEM] + [VMEM] * 5, [], flops, 6 * MIB
    )(pos, wbt, slope, c_own, c_p, c_n)
    gr_p, gr_n = both(grad)

    quarter = n // (tm // LISTED)
    video, send = call(
        video_kernel,
        (rows(n), jax.ShapeDtypeStruct((tm, ch // 2 + quarter, width), BF16)),
        [SMEM, SMEM] + [VMEM] * 8,
        [
            pltpu.VMEM((n + 2, ch, width), BF16),
            pltpu.VMEM((n, width), F32),
        ],
        flops * 4 // 3,
        6 * MIB,
    )(pos, listed, wb, wp, plane_row, pool, v_own, inner, in_p, in_n)
    recv = lax.all_to_all(send, "tm", split_axis=0, concat_axis=0, tiled=True)
    wide = jax.ShapeDtypeStruct((n, ch, width), F32)
    part, rise = call(near_kernel, (wide, wide), [VMEM] * 5, [], flops * 2 // 3, 8 * MIB)(
        wat, gr_p, grad, c, v
    )
    input_grad = call(input_grad_kernel, rows(n), [VMEM] * 4, [], flops // 3, 6 * MIB)(
        wat, part, rise, gr_n
    )
    plane_scores, time_scores = call(
        time_kernel_body,
        (jax.ShapeDtypeStruct((quarter, width), F32), jax.ShapeDtypeStruct((1, width // 2), F32)),
        [SMEM, SMEM, VMEM, VMEM, VMEM, VMEM],
        [],
        flops // 20,
        MIB,
    )(pos, listed, wt, mixer, time_row, recv)
    return (video[None], input_grad[None], plane_scores[None, None], time_scores[None])


def solution(mesh):
    return jax.shard_map(
        shards,
        mesh=mesh,
        in_specs=(P("tm", "space", None, None), P("tm", "space", None, None)) + (P(),) * 8,
        out_specs=(
            P("tm", "space", None, None),
            P("tm", "space", None, None),
            P("tm", "space", None, None),
            P("space", "tm", None),
        ),
        check_vma=False,
    )
```
